32 devices in a mesh: rows: 8 (over y, x, core), tiles: 4 (over z).
Axes of the slice: x: 2, y: 2, z: 4, core: 2. Of those that a mesh axis runs over, the one named last changes fastest.
Arguments:
- embedding: bfloat16 [16384, 256], P('rows'), may hold values from -6 to 6
- start_block: float32 [64, 16384], P(None, ('rows', 'tiles')), may hold values from -4000 to 4000
- start_step: float32 [64, 16384], P(None, ('rows', 'tiles')), may hold values from -4000 to 4000
- rotations: float32 [2, 192, 64], replicated, may hold values from -0.4375 to 0.4375
- neighbour_cols: int32 [128, 48], P('rows', 'tiles'), may hold values from 0 to 127, as said below
- tile_counts: int32 [128], P('rows'), may hold values from 1 to 48, as said below
Outputs:
- block_out: float32 [64, 16384], P(None, ('rows', 'tiles'))
- step_out: float32 [64, 16384], P(None, ('rows', 'tiles'))
The draws below stay inside these ranges and needn't reach their ends.
Inputs may be any that keep to these rules, and one draw needn't show every extreme that they name: `neighbour_cols`: slot 0 of row block b is b itself; slots 1 to tile_counts[b] - 1 hold distinct blocks c with 0 < |c - b| <= 32; later slots hold b or such blocks and are not used. `tile_counts`: at most the number of blocks c with |c - b| <= 32; 48 in some block of every draw.
All inputs are finite; a program needn't handle non-finite values.
Results may differ from the reference program's by a relative error of at most 0.007.
The reference program's roundings to bfloat16 on the way count: a program that leaves them out, or rounds other values in their place, can miss the bound.
Values may be sent and summed in bfloat16 or wider, within the bound.
No kernel may reach another device: no remote copies, remote signals or barrier semaphores. Data moves between devices by JAX's collectives and lax.ppermute only.
A program may use at most 64 MiB of HBM per device.

```python
import jax
import jax.numpy as jnp
from jax import lax

EMB = 256
K = 64
BR = 128
BLK_DEV = 16
MAXT = 48
REACH = 2
ITERS = 2
BLOCKS = 128
ROWS = 16384


def spread_field(noise, key):
    row_key, col_key = jax.random.split(key)
    position = jnp.arange(ROWS, dtype=jnp.float32) / ROWS
    row_scale = 3.0 ** position[None, :] * 10.0 ** jax.random.uniform(row_key, (1, ROWS))
    col_scale = 10.0 ** jax.random.uniform(col_key, (K, 1))
    return (jnp.clip(noise, -4.0, 4.0) * row_scale * col_scale).astype(jnp.float32)


def draw_start_block(key, part):
    key = jax.random.fold_in(key, 5)
    noise_key = jax.random.fold_in(key, 0)
    scale_key = jax.random.fold_in(key, 2)
    noise = jax.random.normal(noise_key, (K, ROWS))
    return spread_field(noise, scale_key)


def draw_start_step(key, part):
    key = jax.random.fold_in(key, 7)
    noise_key = jax.random.fold_in(key, 0)
    scale_key = jax.random.fold_in(key, 2)
    noise = jax.random.normal(noise_key, (K, ROWS))
    return spread_field(noise, scale_key)


def draw_neighbour_cols(key, part):
    key = jax.random.fold_in(key, 13)
    reach = REACH * BLK_DEV
    blocks = jnp.arange(BLOCKS, dtype=jnp.int32)[:, None]
    offsets = jnp.concatenate([jnp.arange(-reach, 0, dtype=jnp.int32), jnp.arange(1, reach + 1, dtype=jnp.int32)])
    target = blocks + offsets[None, :]
    valid = (target >= 0) & (target < BLOCKS)
    draws = jax.random.randint(key, (BLOCKS, 2 * reach), 0, 1 << 20)
    scores = jnp.where(valid, draws, 1 << 21) * (2 * reach) + jnp.arange(2 * reach, dtype=jnp.int32)[None, :]
    order = jnp.argsort(scores, axis=1, stable=True)[:, :MAXT - 1]
    chosen = jnp.take_along_axis(target, order, axis=1)
    usable = jnp.take_along_axis(valid, order, axis=1)
    rest = jnp.where(usable, chosen, blocks)
    return jnp.concatenate([blocks, rest], axis=1).astype(jnp.int32)


def draw_tile_counts(key, part):
    key = jax.random.fold_in(key, 11)
    pick_key, level_key = jax.random.split(key)
    reach = REACH * BLK_DEV
    blocks = jnp.arange(BLOCKS, dtype=jnp.int32)
    room = jnp.minimum(blocks, reach) + jnp.minimum(BLOCKS - 1 - blocks, reach) + 1
    level = jax.random.randint(level_key, (BLOCKS,), 0, 64)
    wanted = 1 + (MAXT - 1) * level * level * level // (63 * 63 * 63)
    full_block = jax.random.randint(pick_key, (), reach, BLOCKS - reach)
    wanted = jnp.where(blocks == full_block, MAXT, wanted)
    return jnp.minimum(wanted, room).astype(jnp.int32)


def level_of(rng, extent, shards, smallest, top_value):
    level, own = 1.0, jax.random.fold_in(rng, 6)
    for dim, parts in shards:
        steps = jnp.exp(jax.random.uniform(jax.random.fold_in(own, dim), (parts,), jnp.float32, smallest / len(shards), top_value / len(shards)))
        level = level * jnp.repeat(steps, extent[dim] // parts).reshape([-1 if axis == dim else 1 for axis in range(len(extent))])
    return level


def centred(stream_key, extent, width, most, cuts=(), kind=jnp.bfloat16):
    factor_of = level_of(stream_key, extent, cuts, -0.22, 0.18) if cuts else 1.0
    drawn = jax.random.normal(stream_key, extent, jnp.float32) * width * factor_of
    return jnp.minimum(jnp.maximum(drawn, -most), most).astype(kind)


def setup_inputs(seed: int = 0) -> dict:
    seeds = jax.random.split(jax.random.key(seed), 7)
    return {
        "embedding": centred(seeds[0], (ROWS, EMB), 1.0, 6.0, ((0, 8),)),
        "start_block": draw_start_block(jax.random.fold_in(seeds[6], 71), 0),
        "start_step": draw_start_step(jax.random.fold_in(seeds[6], 71), 0),
        "rotations": centred(seeds[3], (ITERS, 3 * K, K), (3 * K) ** -0.5, 0.4375, (), jnp.float32),
        "neighbour_cols": draw_neighbour_cols(jax.random.fold_in(seeds[6], 71), 0),
        "tile_counts": draw_tile_counts(jax.random.fold_in(seeds[6], 71), 0),
    }


TAU = 6.0
EPS = 1e-06
PRECISE = lax.Precision.HIGHEST

def normalize_rows(embedding):
    values = embedding.astype(jnp.float32)
    factor = lax.rsqrt(lax.optimization_barrier(jnp.mean(values * values, axis=1, keepdims=True)) + EPS)
    return (values * factor).astype(jnp.bfloat16)

def rms_rows(values):
    return jnp.sqrt(lax.optimization_barrier(jnp.mean(values * values, axis=1)) + EPS)

def graph_product(unit_rows, vectors, neighbour_cols, tile_counts):
    blocks_all = unit_rows.astype(jnp.float32).reshape(BLOCKS, BR, EMB)
    vec_blocks = vectors.reshape(K, BLOCKS, BR)

    def add_slot(running, which_slot):
        col_index = lax.dynamic_index_in_dim(neighbour_cols, which_slot, 1, keepdims=False)
        partner = jnp.take(blocks_all, col_index, axis=0)
        scores = jnp.einsum('bie,bje->bij', blocks_all, partner, precision=PRECISE)
        slot_mask = (which_slot < tile_counts).astype(jnp.float32) / (BR * MAXT)
        weights = jnp.exp(scores * (TAU / EMB)) * slot_mask[:, None, None]
        inputs = jnp.take(vec_blocks, col_index, axis=1)
        return (running + jnp.einsum('bij,kbj->kbi', weights, inputs, precision=PRECISE), None)
    running, unused = lax.scan(add_slot, jnp.zeros((K, BLOCKS, BR), jnp.float32), jnp.arange(MAXT, dtype=jnp.int32))
    return running.reshape(K, ROWS)

def reference(embedding, start_block, start_step, rotations, neighbour_cols, tile_counts):
    unit_rows = normalize_rows(embedding)
    vectors = start_block / rms_rows(start_block)[:, None]
    steps = start_step / rms_rows(start_step)[:, None]
    for iteration in range(ITERS):
        image = graph_product(unit_rows, vectors, neighbour_cols, tile_counts)
        rayleigh = jnp.dot(vectors, image.T, precision=PRECISE) / ROWS
        resid = image - jnp.dot(rayleigh.T, vectors, precision=PRECISE)
        resid_unit = resid / rms_rows(resid)[:, None]
        basis = jnp.concatenate([vectors, resid_unit, steps], axis=0)
        rotation = rotations[iteration]
        combined = jnp.dot(rotation.T, basis, precision=PRECISE)
        new_steps = jnp.dot(rotation[K:].T, basis[K:], precision=PRECISE)
        scale = rms_rows(combined)
        vectors = combined / scale[:, None]
        steps = new_steps / scale[:, None]
    return (vectors, steps)
```

```python
import functools
import math

import jax
import jax.numpy as jnp
from jax import lax
from jax.experimental import pallas as pl
from jax.experimental.pallas import tpu as pltpu
from jax.sharding import PartitionSpec as P

EMB = 256
K = 64
BR = 128
MAXT = 48
REACH = 2
ITERS = 2

TAU = 6.0
EPS = 1e-06
PRECISE = lax.Precision.HIGHEST

WEIGHT = 1.0 / (BR * MAXT)
SIGMA = math.exp(TAU) * WEIGHT
EXP2 = TAU / EMB * math.log2(math.e)
GROUP = 8
SHARDS = 6
F32 = jnp.float32
BF16 = jnp.bfloat16
VMEM = pl.BlockSpec(memory_space=pltpu.VMEM)
SMEM = pl.BlockSpec(memory_space=pltpu.SMEM)


def params():
    return pltpu.CompilerParams(vmem_limit_bytes=48 * 1024 * 1024)


def swapped(value, axis, bits):
    count = lax.axis_size(axis)
    return lax.ppermute(value, axis, [(i, i ^ bits) for i in range(count)])


def rotated(value, axis, steps):
    count = lax.axis_size(axis)
    return lax.ppermute(value, axis, [(i, (i + steps) % count) for i in range(count)])


def other_side(value):
    count = lax.axis_size("rows")
    chips = count // 2
    pairs = []
    for r in range(count):
        chip, core = divmod(r, 2)
        to = (chip + 1) % chips if chip % 2 else (chip - 1) % chips
        pairs.append((r, to * 2 + core))
    return lax.ppermute(value, "rows", pairs)


def chip_halo(value):
    side_a = swapped(value, "rows", 2)
    side_b = other_side(value)
    core = swapped(value, "rows", 1)
    return [
        value, core, side_a, swapped(side_a, "rows", 1), side_b, swapped(side_b, "rows", 1)
    ]


def total_over(value, axis, first):
    count = lax.axis_size(axis)
    bits = first
    while bits < count:
        span = min(4, count // bits)
        value = value + sum(swapped(value, axis, k * bits) for k in range(1, span))
        bits *= span
    return value


def total_over_all(value):
    value = value + swapped(value, "rows", 1)
    value = total_over(value, "rows", 2)
    return total_over(value, "tiles", 1)


def dot_t(a, b):
    return lax.dot_general(a, b, (((1,), (1,)), ((), ())), preferred_element_type=F32)


def unit_of(rows):
    values = rows.astype(F32)
    mean = jnp.sum(values * values, axis=1, keepdims=True) * (1.0 / EMB)
    return (values * lax.rsqrt(mean + EPS)).astype(BF16)


def apply_kernel(blocks, share, devices, *refs):
    meta, items = refs[:2]
    own_emb = refs[2]
    emb = refs[3 : 2 + SHARDS]
    vec = refs[2 + SHARDS : 2 + 2 * SHARDS]
    rest = refs[2 + 2 * SHARDS :]
    own_out, outs = rest[0], rest[1 : 1 + 2 * (devices - 1)]
    diag_out, tiles, unit_own, unit_ext, vec_ext, acc = rest[1 + 2 * (devices - 1) :]
    count, here = meta[0], meta[1]

    @pl.loop(0, blocks)
    def _(b):
        unit_own[b] = unit_of(own_emb[b])

    for i in range(share):
        unit_ext[i] = unit_own[here * share + i]
    for j, ref in enumerate(emb):
        for i in range(share):
            unit_ext[(j + 1) * share + i] = unit_of(ref[pl.ds(i * BR, BR), :])
    for j, ref in enumerate(vec):
        for i in range(share):
            vec_ext[j * share + i] = ref[:, pl.ds(i * BR, BR)]
    acc[...] = jnp.zeros_like(acc)

    rows = lax.broadcasted_iota(jnp.int32, (BR, BR), 0)
    cols = lax.broadcasted_iota(jnp.int32, (BR, BR), 1)
    for i in range(share):
        unit = unit_ext[i]
        weights = jnp.exp2(dot_t(unit, unit) * EXP2)
        on_diag = rows == cols
        diag_out[:, pl.ds(i * BR, BR)] = jnp.sum(
            jnp.where(on_diag, weights, 0.0), axis=0, keepdims=True
        )
        off = jnp.where(on_diag, 0.0, weights).astype(BF16)
        tiles[i] = off
        acc[here * share + i] = jnp.dot(vec_ext[i], off, preferred_element_type=F32)

    @pl.loop(0, (count + GROUP - 1) // GROUP)
    def _(step):
        picked = []
        for g in range(GROUP):
            at = step * GROUP + g
            flat = items[at]
            ext, own = flat // blocks, flat % blocks
            picked.append((ext, own, jnp.where(at < count, own, blocks)))
        scores = [dot_t(unit_ext[ext], unit_own[own]) for ext, own, _ in picked]
        weights = [jnp.exp2(s * EXP2).astype(BF16) for s in scores]
        for g in range(GROUP):
            tiles[share + step * GROUP + g] = weights[g]
        parts = [
            jnp.dot(vec_ext[ext], w, preferred_element_type=F32)
            for (ext, _, _), w in zip(picked, weights)
        ]
        for (_, _, to), part in zip(picked, parts):
            acc[to] += part

    for j in range(devices):
        first = lax.rem(here + j, devices) * share
        for i in range(share):
            part = acc[first + i]
            at = pl.ds(i * BR, BR)
            if j == 0:
                own_out[:, at] = part
            else:
                outs[2 * (j - 1)][:, at] = part[:K].astype(BF16)
                outs[2 * (j - 1) + 1][:, at] = part[K:].astype(BF16)


def again_kernel(blocks, share, devices, *refs):
    meta, items, tiles = refs[:3]
    vec = refs[3 : 3 + SHARDS]
    outs = refs[3 + SHARDS : 3 + SHARDS + devices]
    vec_ext, acc = refs[3 + SHARDS + devices :]
    count, here = meta[0], meta[1]
    for j, ref in enumerate(vec):
        for i in range(share):
            vec_ext[j * share + i] = ref[:, pl.ds(i * BR, BR)]
    acc[...] = jnp.zeros_like(acc)
    for i in range(share):
        acc[here * share + i] = jnp.dot(vec_ext[i], tiles[i], preferred_element_type=F32)

    @pl.loop(0, (count + GROUP - 1) // GROUP)
    def _(step):
        picked = []
        for g in range(GROUP):
            at = step * GROUP + g
            flat = items[at]
            picked.append((flat // blocks, jnp.where(at < count, flat % blocks, blocks)))
        parts = [
            jnp.dot(vec_ext[ext], tiles[share + step * GROUP + g], preferred_element_type=F32)
            for g, (ext, _) in enumerate(picked)
        ]
        for (_, to), part in zip(picked, parts):
            acc[to] += part

    for j in range(devices):
        first = lax.rem(here + j, devices) * share
        for i in range(share):
            outs[j][:, pl.ds(i * BR, BR)] = acc[first + i].astype(outs[j].dtype)


def mul(a, b):
    return jnp.dot(a, b, precision=PRECISE, preferred_element_type=F32)


def step_coefficients(g_vv, g_vs, g_ss, g_vj, g_sj, g_jj, rotation, total):
    eye = (
        lax.broadcasted_iota(jnp.int32, (K, K), 0) == lax.broadcasted_iota(jnp.int32, (K, K), 1)
    )
    m = g_vj * (1.0 / total) + SIGMA * (g_vv * (1.0 / total) - eye.astype(F32))
    resid_sq = (
        jnp.sum(jnp.where(eye, g_jj, 0.0), axis=0, keepdims=True)
        - 2.0 * jnp.sum(m * g_vj, axis=0, keepdims=True)
        + jnp.sum(m * mul(g_vv, m), axis=0, keepdims=True)
    )
    resid_inv = 1.0 / jnp.sqrt(jnp.maximum(resid_sq, 0.0) * (1.0 / total) + EPS)
    on_v, on_resid, on_s = rotation[:K].T, rotation[K : 2 * K].T, rotation[2 * K :].T
    p_j = on_resid * resid_inv
    p_step = -mul(p_j, m.T)
    p_v = jnp.concatenate([on_v + p_step, p_step], axis=0)
    p_s, p_j = jnp.concatenate([on_s, on_s], axis=0), jnp.concatenate([p_j, p_j], axis=0)
    g_v = mul(p_v, g_vv) + mul(p_j, g_vj.T) + mul(p_s, g_vs.T)
    g_s = mul(p_v, g_vs) + mul(p_j, g_sj.T) + mul(p_s, g_ss)
    g_j = mul(p_v, g_vj) + mul(p_j, g_jj) + mul(p_s, g_sj)
    comb_sq = jnp.sum((g_v * p_v + g_s * p_s + g_j * p_j)[:K], axis=1, keepdims=True)
    scale = 1.0 / jnp.sqrt(jnp.maximum(comb_sq, 0.0) * (1.0 / total) + EPS)
    scale = jnp.concatenate([scale, scale], axis=0)
    return scale * p_v, scale * p_s, scale * p_j, scale * g_v, scale * g_s, scale * g_j


def gram_kernel(a_ref, b_ref, j_ref, out_ref):
    x, y, j = a_ref[...], b_ref[...], j_ref[...]
    pairs = ((x, x), (x, y), (y, y), (x, j), (y, j), (j, j))
    for n, (a, b) in enumerate(pairs):
        out_ref[n] = lax.dot_general(
            a, b, (((1,), (1,)), ((), ())), precision=PRECISE, preferred_element_type=F32
        )


def first_kernel(total, g_ref, rot_ref, x_ref, y_ref, j_ref, t_ref, v_out, s_out, part_out, c_out, g_out):
    eye = (
        lax.broadcasted_iota(jnp.int32, (K, K), 0) == lax.broadcasted_iota(jnp.int32, (K, K), 1)
    )
    xx, xy, yy, xj, yj, jj = (g_ref[n] for n in range(6))

    def inv_rms(square, axis):
        picked = jnp.sum(jnp.where(eye, square, 0.0), axis=axis, keepdims=True)
        return 1.0 / jnp.sqrt(picked * (1.0 / total) + EPS)

    x_col, x_row = inv_rms(xx, 1), inv_rms(xx, 0)
    y_col, y_row = inv_rms(yy, 1), inv_rms(yy, 0)
    g_vv, g_vs, g_ss = xx * x_col * x_row, xy * x_col * y_row, yy * y_col * y_row
    g_vj, g_sj, g_jj = xj * x_col * x_row, yj * y_col * x_row, jj * x_col * x_row
    p_v, p_s, p_j, g_v, g_s, g_j = step_coefficients(
        g_vv, g_vs, g_ss, g_vj, g_sj, g_jj, rot_ref[...], total
    )
    new = mul(g_v, p_v.T) + mul(g_s, p_s.T) + mul(g_j, p_j.T)
    g_out[0], g_out[1], g_out[2] = new[:K, :K], new[:K, K:], new[K:, K:]
    p_v, p_j, p_s = p_v * x_row, p_j * x_row, p_s * y_row
    x, y, j, t = x_ref[...], y_ref[...], j_ref[...], t_ref[...]
    both = mul(p_v, x) + mul(p_s, y) + mul(p_j, j)
    v_out[...], s_out[...] = both[:K], both[K:]
    part_out[...] = mul(p_v[:K], j) + mul(p_s[:K], t)
    c_out[...] = p_j[:K]


def second_kernel(v_ref, s_ref, part_ref, c_ref, q_ref, j_out, g_out):
    j = part_ref[...] + mul(c_ref[...], q_ref[...])
    j_out[...] = j
    for n, a in enumerate((v_ref[...], s_ref[...], j)):
        g_out[n] = lax.dot_general(
            a, j, (((1,), (1,)), ((), ())), precision=PRECISE, preferred_element_type=F32
        )


def last_kernel(total, g_ref, h_ref, rot_ref, v_ref, s_ref, j_ref, v_out, s_out):
    p_v, p_s, p_j, _, _, _ = step_coefficients(
        g_ref[0], g_ref[1], g_ref[2], h_ref[0], h_ref[1], h_ref[2], rot_ref[...], total
    )
    both = mul(p_v, v_ref[...]) + mul(p_s, s_ref[...]) + mul(p_j, j_ref[...])
    v_out[...], s_out[...] = both[:K], both[K:]


def call(kernel, outs, *args, smem=0, scratch=(), out_specs=None):
    return pl.pallas_call(
        kernel,
        out_shape=tuple(jax.ShapeDtypeStruct(shape, dtype) for shape, dtype in outs),
        in_specs=[SMEM] * smem + [VMEM] * (len(args) - smem),
        out_specs=tuple(out_specs or [VMEM] * len(outs)),
        scratch_shapes=list(scratch),
        compiler_params=params(),
    )(*args)


def tile_list(cols, counts, here, row, share, devices):
    blocks, span = cols.shape
    flat = blocks * SHARDS * share
    used = []
    for step in range(devices):
        part = cols if step == 0 else rotated(cols, "tiles", step)
        first = lax.rem(here - step + devices, devices) * span
        slot = first + lax.broadcasted_iota(jnp.int32, (blocks, span), 1)
        used.append((part, slot))
    col = jnp.concatenate([part for part, _ in used], axis=1)
    slot = jnp.concatenate([s for _, s in used], axis=1)
    block = row * blocks + lax.broadcasted_iota(jnp.int32, col.shape, 0)
    shard, inner = col // blocks, col % blocks
    other_core = (shard % 2 != row % 2).astype(jnp.int32)
    chip, own_chip = shard // 2, row // 2
    place = other_core + jnp.where(chip == own_chip, 0, jnp.where(chip == own_chip ^ 1, 2, 4))
    mine = (slot < counts[:, None]) & (inner // share == here) & (col != block)
    ext = jnp.where(mine, place * share + inner % share, -1)
    wanted = lax.broadcasted_iota(jnp.int32, (SHARDS * share, blocks, 1), 0)
    mask = jnp.any(ext[None] == wanted, axis=2).astype(F32).reshape(flat)
    index = jnp.arange(flat, dtype=jnp.int32)
    before = (index[:, None] < index[None, :]).astype(F32)
    place = jnp.dot(mask, before).astype(jnp.int32)
    hit = (place[:, None] == index[None, :]) & (mask[:, None] > 0)
    items = jnp.sum(jnp.where(hit, index[:, None], 0), axis=0)
    count = jnp.sum(mask).astype(jnp.int32)
    return jnp.concatenate([items, jnp.zeros((GROUP,), jnp.int32)]), jnp.stack([count, here])


def local(embedding, start_block, start_step, rotations, neighbour_cols, tile_counts):
    devices = lax.axis_size("tiles")
    width = start_block.shape[1]
    share = width // BR
    blocks = tile_counts.shape[0]
    total = width * devices * lax.axis_size("rows")
    here, row = lax.axis_index("tiles"), lax.axis_index("rows")
    flat = blocks * SHARDS * share

    own_emb = lax.dynamic_slice_in_dim(embedding, here * width, width, 0)
    emb = chip_halo(own_emb)
    vec = chip_halo(jnp.concatenate([start_block, start_step], axis=0).astype(BF16))
    items, meta = tile_list(neighbour_cols, tile_counts, here, row, share, devices)

    tiles_shape = ((share + flat + GROUP, BR, BR), BF16)
    outs = call(
        functools.partial(apply_kernel, blocks, share, devices),
        [((2 * K, width), F32)]
        + [((K, width), BF16)] * (2 * (devices - 1))
        + [((1, width), F32), tiles_shape],
        meta,
        items,
        embedding.reshape(blocks, BR, EMB),
        *emb[1:],
        *vec,
        smem=2,
        scratch=[
            pltpu.VMEM((blocks, BR, EMB), BF16),
            pltpu.VMEM((SHARDS * share, BR, EMB), BF16),
            pltpu.VMEM((SHARDS * share, 2 * K, BR), BF16),
            pltpu.VMEM((blocks + 1, 2 * K, BR), F32),
        ],
    )
    own, sent, diag, tiles = outs[0], outs[1:-2], outs[-2], outs[-1]
    diag = diag * WEIGHT - SIGMA

    def collect(own_part, parts, vectors):
        got = own_part
        for n, part in enumerate(parts):
            got = got + rotated(part, "tiles", n + 1).astype(F32)
        return got * WEIGHT + diag * vectors

    image = collect(own[:K], sent[0::2], start_block)
    image_vec = chip_halo(image.astype(BF16))
    step_image = collect(own[K:], sent[1::2], start_step)

    gram = total_over_all(
        call(gram_kernel, [((6, K, K), F32)], start_block, start_step, image)[0]
    )
    vectors, steps, part, coef, gram = call(
        functools.partial(first_kernel, total),
        [((K, width), F32)] * 3 + [((K, K), F32), ((3, K, K), F32)],
        gram,
        rotations[0],
        start_block,
        start_step,
        image,
        step_image,
    )

    outs = call(
        functools.partial(again_kernel, blocks, share, devices),
        [((K, width), F32)] + [((K, width), BF16)] * (devices - 1),
        meta,
        items,
        tiles,
        *image_vec,
        smem=2,
        scratch=[
            pltpu.VMEM((SHARDS * share, K, BR), BF16),
            pltpu.VMEM((blocks + 1, K, BR), F32),
        ],
    )
    twice = collect(outs[0], outs[1:], image)
    image, products = call(
        second_kernel,
        [((K, width), F32), ((3, K, K), F32)],
        vectors,
        steps,
        part,
        coef,
        twice,
    )
    products = total_over_all(products)
    return call(
        functools.partial(last_kernel, total),
        [((K, width), F32)] * 2,
        gram,
        products,
        rotations[1],
        vectors,
        steps,
        image,
    )


def solution(mesh):
    return jax.shard_map(
        local,
        mesh=mesh,
        in_specs=(
            P("rows", None),
            P(None, ("rows", "tiles")),
            P(None, ("rows", "tiles")),
            P(),
            P("rows", "tiles"),
            P("rows"),
        ),
        out_specs=(P(None, ("rows", "tiles")), P(None, ("rows", "tiles"))),
        check_vma=False,
    )
```

```python
import functools
import math

import jax
import jax.numpy as jnp
from jax import lax
from jax.experimental import pallas as pl
from jax.experimental.pallas import tpu as pltpu
from jax.sharding import PartitionSpec as P

EMB = 256
K = 64
BR = 128
MAXT = 48
REACH = 2
ITERS = 2

TAU = 6.0
EPS = 1e-06
PRECISE = lax.Precision.HIGHEST

WEIGHT = 1.0 / (BR * MAXT)
SIGMA = math.exp(TAU) * WEIGHT
EXP2 = TAU / EMB * math.log2(math.e)
GROUP = 8
SHARDS = 6
F32 = jnp.float32
BF16 = jnp.bfloat16
VMEM = pl.BlockSpec(memory_space=pltpu.VMEM)
SMEM = pl.BlockSpec(memory_space=pltpu.SMEM)


def swapped(value, axis, bits):
    count = lax.axis_size(axis)
    return lax.ppermute(value, axis, [(i, i ^ bits) for i in range(count)])


def rotated(value, axis, steps):
    count = lax.axis_size(axis)
    return lax.ppermute(value, axis, [(i, (i + steps) % count) for i in range(count)])


def other_side(value):
    count = lax.axis_size("rows")
    chips = count // 2
    pairs = []
    for r in range(count):
        chip, core = divmod(r, 2)
        to = (chip + 1) % chips if chip % 2 else (chip - 1) % chips
        pairs.append((r, to * 2 + core))
    return lax.ppermute(value, "rows", pairs)


def after(value, *others):
    return lax.optimization_barrier((value, *others))[0]


def across(value):
    return swapped(value, "rows", 2), other_side(value), swapped(value, "rows", 1)


def by_core(side_a, side_b):
    return [side_a, swapped(side_a, "rows", 1), side_b, swapped(side_b, "rows", 1)]


def chip_sum_part(value, part):
    rows, tiles = lax.axis_size("rows"), lax.axis_size("tiles")
    if rows // 2 == tiles == 4:
        parts = [value]
        for step in range(1, 4):
            pairs = []
            for r in range(rows):
                for t in range(tiles):
                    along_rows = r % 2 == part
                    to = (r ^ (2 * step), t) if along_rows else (r, (t + step) % tiles)
                    pairs.append((r * tiles + t, to[0] * tiles + to[1]))
            parts.append(lax.ppermute(value, ("rows", "tiles"), pairs))
        return sum(parts)
    if part == 0:
        return value + sum(rotated(value, "tiles", n) for n in range(1, tiles))
    bits = 2
    while bits < rows:
        span = min(4, rows // bits)
        value = value + sum(swapped(value, "rows", k * bits) for k in range(1, span))
        bits *= span
    return value


def dot_t(a, b):
    return lax.dot_general(a, b, (((1,), (1,)), ((), ())), preferred_element_type=F32)


def dot_exact(a, b):
    return lax.dot_general(
        a, b, (((1,), (1,)), ((), ())), precision=PRECISE, preferred_element_type=F32
    )


def unit_of(rows):
    values = rows.astype(F32)
    mean = jnp.sum(values * values, axis=1, keepdims=True) * (1.0 / EMB)
    return (values * lax.rsqrt(mean + EPS)).astype(BF16)


def pack_kernel(meta, emb, block, step, cols, emb_out, vec_out, cols_out, block_buf, step_buf, sems):
    here, width = meta[0], emb_out.shape[0]
    copies = [
        pltpu.make_async_copy(emb.at[pl.ds(here * width, width), :], emb_out, sems.at[0]),
        pltpu.make_async_copy(block, block_buf, sems.at[1]),
        pltpu.make_async_copy(step, step_buf, sems.at[2]),
    ]
    for copy in copies:
        copy.start()
    cols_out[...] = cols[...]
    copies[1].wait()
    vec_out[:K, :] = block_buf[...].astype(BF16)
    copies[2].wait()
    vec_out[K:, :] = step_buf[...].astype(BF16)
    copies[0].wait()


def group_copies(count, first, source, target, sems, body):
    @pl.loop(0, (count + GROUP - 1) // GROUP)
    def _(step):
        at = pl.ds(first + step * GROUP, GROUP)
        body(pltpu.make_async_copy(source.at[at], target.at[at], sems.at[step]))


def build_tiles(blocks, first, items, unit_own, unit_ext, tiles, tiles_out, sems):
    count = items[items.shape[0] - 1]

    @pl.loop(0, (count + GROUP - 1) // GROUP)
    def _(step):
        picked = [items[step * GROUP + g] for g in range(GROUP)]
        scores = [dot_t(unit_ext[f // blocks], unit_own[f % blocks]) for f in picked]
        for g in range(GROUP):
            tiles[first + step * GROUP + g] = jnp.exp2(scores[g] * EXP2).astype(BF16)
        at = pl.ds(first + step * GROUP, GROUP)
        pltpu.make_async_copy(tiles.at[at], tiles_out.at[at], sems.at[step]).start()

    group_copies(count, first, tiles, tiles_out, sems, lambda copy: copy.wait())


def unit_kernel(emb, unit, buf, sems):
    blocks, parts = unit.shape[0], sems.shape[0]
    each = blocks // parts
    copies = [
        pltpu.make_async_copy(
            emb.at[pl.ds(n * each, each)], buf.at[pl.ds(n * each, each)], sems.at[n]
        )
        for n in range(parts)
    ]
    for copy in copies:
        copy.start()
    for n, copy in enumerate(copies):
        copy.wait()

        @pl.loop(n * each, (n + 1) * each)
        def _(b):
            unit[b] = unit_of(buf[b])


def near_kernel(
    blocks, share, meta, items, unit_own, emb_core, diag_out, tiles_out, unit_ext, tiles, sems
):
    here = meta[0]
    for i in range(share):
        unit_ext[i] = unit_own[here * share + i]
        unit_ext[share + i] = unit_of(emb_core[pl.ds(i * BR, BR), :])
    rows = lax.broadcasted_iota(jnp.int32, (BR, BR), 0)
    cols = lax.broadcasted_iota(jnp.int32, (BR, BR), 1)
    for i in range(share):
        unit = unit_ext[i]
        weights = jnp.exp2(dot_t(unit, unit) * EXP2)
        on_diag = rows == cols
        diag_out[:, pl.ds(i * BR, BR)] = (
            jnp.sum(jnp.where(on_diag, weights, 0.0), axis=0, keepdims=True) * WEIGHT - SIGMA
        )
        tiles[i] = jnp.where(on_diag, 0.0, weights).astype(BF16)
    at = pl.ds(0, share)
    copy = pltpu.make_async_copy(tiles.at[at], tiles_out.at[at], sems.at[sems.shape[0] - 1])
    copy.start()
    build_tiles(blocks, share, items, unit_own, unit_ext, tiles, tiles_out, sems)
    copy.wait()


def far_kernel(blocks, share, meta, items, unit_own, *refs):
    emb, (tiles_out, unit_ext, tiles, sems) = refs[:-4], refs[-4:]
    for j, ref in enumerate(emb):
        for i in range(share):
            unit_ext[j * share + i] = unit_of(ref[pl.ds(i * BR, BR), :])
    build_tiles(blocks, 0, items, unit_own, unit_ext, tiles, tiles_out, sems)


def apply_kernel(blocks, share, devices, *refs):
    meta, items, stored = refs[0], refs[1:3], refs[3:5]
    vec, outs = refs[5 : 5 + SHARDS], refs[5 + SHARDS : -6]
    vec_ext, acc, tiles, sems = refs[-6], refs[-5], refs[-4:-2], refs[-2:]
    here = meta[0]
    counts = [ref[ref.shape[0] - 1] for ref in items]
    firsts = (share, 0)
    at = pl.ds(0, share)
    diag_copy = pltpu.make_async_copy(
        stored[0].at[at], tiles[0].at[at], sems[0].at[sems[0].shape[0] - 1]
    )
    diag_copy.start()
    for part in range(2):
        group_copies(
            counts[part], firsts[part], stored[part], tiles[part], sems[part],
            lambda copy: copy.start(),
        )
    for j, ref in enumerate(vec):
        for i in range(share):
            vec_ext[j * share + i] = ref[:, pl.ds(i * BR, BR)]
    acc[...] = jnp.zeros_like(acc)
    diag_copy.wait()
    for i in range(share):
        acc[here * share + i] = jnp.dot(vec_ext[i], tiles[0][i], preferred_element_type=F32)
    for part in range(2):
        count, first, base = counts[part], firsts[part], (0, 2 * share)[part]

        @pl.loop(0, (count + GROUP - 1) // GROUP)
        def _(step):
            group = pl.ds(first + step * GROUP, GROUP)
            pltpu.make_async_copy(
                stored[part].at[group], tiles[part].at[group], sems[part].at[step]
            ).wait()
            picked = []
            for g in range(GROUP):
                at = step * GROUP + g
                flat = items[part][at]
                picked.append(
                    (base + flat // blocks, jnp.where(at < count, flat % blocks, blocks))
                )
            parts = [
                jnp.dot(
                    vec_ext[ext],
                    tiles[part][first + step * GROUP + g],
                    preferred_element_type=F32,
                )
                for g, (ext, _) in enumerate(picked)
            ]
            for (_, to), value in zip(picked, parts):
                acc[to] += value

    for n, out in enumerate(outs):
        rows = pl.ds(n // devices * K, K)
        at_block = lax.rem(here + n % devices, devices) * share
        for i in range(share):
            value = acc[at_block + i, rows, :] * WEIGHT
            out[:, pl.ds(i * BR, BR)] = value.astype(out.dtype)


def summed(parts, diag, vectors):
    value = parts[0][...] + diag[...] * vectors
    for ref in parts[1:]:
        value = value + ref[...].astype(F32)
    return value


def image_kernel(devices, *refs):
    parts, (diag, vec, out, out_half) = refs[:devices], refs[devices:]
    value = summed(parts, diag, vec[...])
    out[...] = value
    out_half[...] = value.astype(BF16)


def mul(a, b):
    return jnp.dot(a, b, precision=PRECISE, preferred_element_type=F32)


def step_coefficients(g_vv, g_vs, g_ss, g_vj, g_sj, g_jj, rotation, total):
    eye = (
        lax.broadcasted_iota(jnp.int32, (K, K), 0) == lax.broadcasted_iota(jnp.int32, (K, K), 1)
    )
    m = g_vj * (1.0 / total) + SIGMA * (g_vv * (1.0 / total) - eye.astype(F32))
    resid_sq = (
        jnp.sum(jnp.where(eye, g_jj, 0.0), axis=0, keepdims=True)
        - 2.0 * jnp.sum(m * g_vj, axis=0, keepdims=True)
        + jnp.sum(m * mul(g_vv, m), axis=0, keepdims=True)
    )
    resid_inv = 1.0 / jnp.sqrt(jnp.maximum(resid_sq, 0.0) * (1.0 / total) + EPS)
    on_v, on_resid, on_s = rotation[:K].T, rotation[K : 2 * K].T, rotation[2 * K :].T
    p_j = on_resid * resid_inv
    p_step = -mul(p_j, m.T)
    p_v = jnp.concatenate([on_v + p_step, p_step], axis=0)
    p_s, p_j = jnp.concatenate([on_s, on_s], axis=0), jnp.concatenate([p_j, p_j], axis=0)
    g_v = mul(p_v, g_vv) + mul(p_j, g_vj.T) + mul(p_s, g_vs.T)
    g_s = mul(p_v, g_vs) + mul(p_j, g_sj.T) + mul(p_s, g_ss)
    g_j = mul(p_v, g_vj) + mul(p_j, g_jj) + mul(p_s, g_sj)
    comb_sq = jnp.sum((g_v * p_v + g_s * p_s + g_j * p_j)[:K], axis=1, keepdims=True)
    scale = 1.0 / jnp.sqrt(jnp.maximum(comb_sq, 0.0) * (1.0 / total) + EPS)
    scale = jnp.concatenate([scale, scale], axis=0)
    return scale * p_v, scale * p_s, scale * p_j, scale * g_v, scale * g_s, scale * g_j


def gram_kernel(x_ref, y_ref, j_ref, out):
    x, y, j = x_ref[...], y_ref[...], j_ref[...]
    for n, (a, b) in enumerate(((x, x), (x, y), (y, y), (x, j), (y, j), (j, j))):
        out[n] = dot_exact(a, b)


def first_kernel(devices, total, rot_ref, x_ref, y_ref, j_ref, diag, gram, *refs):
    parts, outs = refs[:devices], refs[devices:]
    v_out, s_out, part_out, c_out, g_out = outs
    eye = (
        lax.broadcasted_iota(jnp.int32, (K, K), 0) == lax.broadcasted_iota(jnp.int32, (K, K), 1)
    )
    xx, xy, yy, xj, yj, jj = (gram[n] for n in range(6))

    def inv_rms(square, axis):
        picked = jnp.sum(jnp.where(eye, square, 0.0), axis=axis, keepdims=True)
        return 1.0 / jnp.sqrt(picked * (1.0 / total) + EPS)

    x_col, x_row = inv_rms(xx, 1), inv_rms(xx, 0)
    y_col, y_row = inv_rms(yy, 1), inv_rms(yy, 0)
    g_vv, g_vs, g_ss = xx * x_col * x_row, xy * x_col * y_row, yy * y_col * y_row
    g_vj, g_sj, g_jj = xj * x_col * x_row, yj * y_col * x_row, jj * x_col * x_row
    p_v, p_s, p_j, g_v, g_s, g_j = step_coefficients(
        g_vv, g_vs, g_ss, g_vj, g_sj, g_jj, rot_ref[...], total
    )
    new = mul(g_v, p_v.T) + mul(g_s, p_s.T) + mul(g_j, p_j.T)
    g_out[0], g_out[1], g_out[2] = new[:K, :K], new[:K, K:], new[K:, K:]
    p_v, p_j, p_s = p_v * x_row, p_j * x_row, p_s * y_row
    x, y, j = x_ref[...], y_ref[...], j_ref[...]
    t = summed(parts, diag, y)
    both = mul(p_v, x) + mul(p_s, y) + mul(p_j, j)
    v_out[...], s_out[...] = both[:K], both[K:]
    part_out[...] = mul(p_v[:K], j) + mul(p_s[:K], t)
    c_out[...] = p_j[:K]


def second_kernel(devices, v_ref, s_ref, part_ref, c_ref, first_ref, diag, *refs):
    parts, (j_out, out) = refs[:devices], refs[devices:]
    j = part_ref[...] + mul(c_ref[...], summed(parts, diag, first_ref[...]))
    j_out[...] = j
    for n, a in enumerate((v_ref[...], s_ref[...], j)):
        out[n] = dot_exact(a, j)


def last_kernel(total, g_ref, rot_ref, v_ref, s_ref, j_ref, h_ref, v_out, s_out):
    p_v, p_s, p_j, _, _, _ = step_coefficients(
        g_ref[0], g_ref[1], g_ref[2], h_ref[0], h_ref[1], h_ref[2], rot_ref[...], total
    )
    both = mul(p_v, v_ref[...]) + mul(p_s, s_ref[...]) + mul(p_j, j_ref[...])
    v_out[...], s_out[...] = both[:K], both[K:]


def call(kernel, outs, *args, smem=0, hbm=0, scratch=(), us=0.0):
    any_memory = pl.BlockSpec(memory_space=pl.ANY)
    args = [
        pltpu.with_memory_space_constraint(arg, pltpu.HBM) if smem <= n < smem + hbm else arg
        for n, arg in enumerate(args)
    ]
    return pl.pallas_call(
        kernel,
        out_shape=tuple(
            pltpu.HBM(*out[:2]) if len(out) > 2 else jax.ShapeDtypeStruct(*out) for out in outs
        ),
        in_specs=[SMEM] * smem + [any_memory] * hbm + [VMEM] * (len(args) - smem - hbm),
        out_specs=tuple(any_memory if len(out) > 2 else VMEM for out in outs),
        scratch_shapes=list(scratch),
        compiler_params=pltpu.CompilerParams(vmem_limit_bytes=24 * 1024 * 1024),
        cost_estimate=pl.CostEstimate(
            flops=int(us * 1e9), bytes_accessed=0, transcendentals=0
        ),
    )(*args)


def tile_list(cols, counts, here, row, share, devices):
    blocks, span = cols[0].shape
    used = []
    for step, part in enumerate(cols):
        first = lax.rem(here - step + devices, devices) * span
        slot = first + lax.broadcasted_iota(jnp.int32, (blocks, span), 1)
        used.append((part, slot))
    col = jnp.concatenate([part for part, _ in used], axis=1)
    slot = jnp.concatenate([s for _, s in used], axis=1)
    block = row * blocks + lax.broadcasted_iota(jnp.int32, col.shape, 0)
    shard, inner = col // blocks, col % blocks
    other_core = (shard % 2 != row % 2).astype(jnp.int32)
    chip, own_chip = shard // 2, row // 2
    place = other_core + jnp.where(chip == own_chip, 0, jnp.where(chip == own_chip ^ 1, 2, 4))
    mine = (slot < counts[:, None]) & (inner // share == here) & (col != block)
    ext = jnp.where(mine, place * share + inner % share, -1)
    wanted = lax.broadcasted_iota(jnp.int32, (SHARDS * share, blocks, 1), 0)
    mask = jnp.any(ext[None] == wanted, axis=2).astype(F32)
    lists = []
    for part in (mask[: 2 * share], mask[2 * share :]):
        flat = part.size
        part = part.reshape(flat)
        index = jnp.arange(flat, dtype=jnp.int32)
        upto = (index[:, None] <= index[None, :]).astype(F32)
        place = jnp.dot(part, upto).astype(jnp.int32)
        wide = jnp.arange(flat + GROUP + 1, dtype=jnp.int32)[None, :]
        used = part[:, None] > 0
        hit = (place[:, None] == wide + 1) & used
        last = (wide == flat + GROUP) & used
        lists.append(jnp.sum(jnp.where(hit, index[:, None], last.astype(jnp.int32)), axis=0))
    return lists


def local(embedding, start_block, start_step, rotations, neighbour_cols, tile_counts):
    devices = lax.axis_size("tiles")
    width = start_block.shape[1]
    share = width // BR
    blocks = tile_counts.shape[0]
    total = width * devices * lax.axis_size("rows")
    here, row = lax.axis_index("tiles"), lax.axis_index("rows")

    meta = here.reshape(1)
    own_emb, own_vec, cols = call(
        pack_kernel,
        [((width, EMB), BF16), ((2 * K, width), BF16), (neighbour_cols.shape, jnp.int32)],
        meta,
        embedding,
        start_block,
        start_step,
        neighbour_cols,
        smem=1,
        hbm=3,
        scratch=[
            pltpu.VMEM((K, width), F32),
            pltpu.VMEM((K, width), F32),
            pltpu.SemaphoreType.DMA((3,)),
        ],
        us=1.0,
    )
    emb_a, emb_b, emb_core = across(own_emb)
    lists = after(cols, emb_core)
    lists = [lists] + [rotated(lists, "tiles", n) for n in range(1, devices)]
    items = tile_list(lists, tile_counts, here, row, share, devices)
    own_vec = after(own_vec, *lists)
    vec_a, vec_b = swapped(own_vec, "rows", 2), other_side(own_vec)

    (unit_own,) = call(
        unit_kernel,
        [((blocks, BR, EMB), BF16)],
        after(embedding.reshape(blocks, BR, EMB), emb_core),
        hbm=1,
        scratch=[pltpu.VMEM((blocks, BR, EMB), BF16), pltpu.SemaphoreType.DMA((4,))],
        us=1.5,
    )
    near, far = 2 * share * blocks, (SHARDS - 2) * share * blocks
    near_shape, far_shape = (share + near + GROUP, BR, BR), (far + GROUP, BR, BR)
    near_sems = pltpu.SemaphoreType.DMA((near // GROUP + 2,))
    far_sems = pltpu.SemaphoreType.DMA((far // GROUP + 1,))
    diag, tiles_near = call(
        functools.partial(near_kernel, blocks, share),
        [((1, width), F32), (near_shape, BF16, "hbm")],
        meta,
        items[0],
        unit_own,
        emb_core,
        smem=2,
        scratch=[
            pltpu.VMEM((2 * share, BR, EMB), BF16),
            pltpu.VMEM(near_shape, BF16),
            near_sems,
        ],
        us=2.0,
    )
    emb_a, emb_b = after(emb_a, diag), after(emb_b, diag)
    (tiles_far,) = call(
        functools.partial(far_kernel, blocks, share),
        [(far_shape, BF16, "hbm")],
        meta,
        items[1],
        unit_own,
        *by_core(emb_a, emb_b),
        smem=2,
        scratch=[
            pltpu.VMEM(((SHARDS - 2) * share, BR, EMB), BF16),
            pltpu.VMEM(far_shape, BF16),
            far_sems,
        ],
        us=2.0,
    )
    vec_core = swapped(after(own_vec, diag), "rows", 1)
    vec = [own_vec, vec_core, *by_core(after(vec_a, tiles_far), after(vec_b, tiles_far))]

    def applied(halo):
        rows = halo[0].shape[0]
        return call(
            functools.partial(apply_kernel, blocks, share, devices),
            ([((K, width), F32)] + [((K, width), BF16)] * (devices - 1)) * (rows // K),
            meta,
            *items,
            tiles_near,
            tiles_far,
            *halo,
            smem=3,
            hbm=2,
            scratch=[
                pltpu.VMEM((SHARDS * share, rows, BR), BF16),
                pltpu.VMEM((blocks + 1, rows, BR), F32),
                pltpu.VMEM(near_shape, BF16),
                pltpu.VMEM(far_shape, BF16),
                near_sems,
                far_sems,
            ],
            us=2.0,
        )

    def gathered(parts):
        return [parts[0]] + [rotated(part, "tiles", n + 1) for n, part in enumerate(parts[1:])]

    parts = applied(vec)
    parts, step_parts = gathered(parts[:devices]), gathered(parts[devices:])
    image, image_half = call(
        functools.partial(image_kernel, devices),
        [((K, width), F32), ((K, width), BF16)],
        *parts,
        diag,
        start_block,
        us=0.1,
    )
    image_a, image_b, image_core = across(image_half)
    (gram,) = call(
        gram_kernel,
        [((6, K, K), F32)],
        start_block,
        start_step,
        after(image, image_core),
        us=0.8,
    )
    image_vec = [image_half, image_core, *by_core(image_a, image_b)]
    gram = gram + swapped(gram, "rows", 1)
    gram = chip_sum_part(after(gram, image_vec[3]), 0)
    parts = applied(image_vec)
    gram = chip_sum_part(after(gram, parts[0]), 1)
    parts = gathered(parts)
    vectors, steps, part, coef, gram = call(
        functools.partial(first_kernel, devices, total),
        [((K, width), F32)] * 3 + [((K, K), F32), ((3, K, K), F32)],
        rotations[0],
        start_block,
        start_step,
        image,
        diag,
        gram,
        *step_parts,
        us=2.8,
    )
    image, products = call(
        functools.partial(second_kernel, devices),
        [((K, width), F32), ((3, K, K), F32)],
        vectors,
        steps,
        part,
        coef,
        image,
        diag,
        *parts,
        us=0.8,
    )
    products = products + swapped(products, "rows", 1)
    products = chip_sum_part(chip_sum_part(products, 0), 1)
    return call(
        functools.partial(last_kernel, total),
        [((K, width), F32)] * 2,
        gram,
        rotations[1],
        vectors,
        steps,
        image,
        products,
        us=2.8,
    )


def solution(mesh):
    return jax.shard_map(
        local,
        mesh=mesh,
        in_specs=(
            P("rows", None),
            P(None, ("rows", "tiles")),
            P(None, ("rows", "tiles")),
            P(),
            P("rows", "tiles"),
            P("rows"),
        ),
        out_specs=(P(None, ("rows", "tiles")), P(None, ("rows", "tiles"))),
        check_vma=False,
    )
```

```python
import functools
import math

import jax
import jax.numpy as jnp
from jax import lax
from jax.experimental import pallas as pl
from jax.experimental.pallas import tpu as pltpu
from jax.sharding import PartitionSpec as P

EMB = 256
K = 64
BR = 128
MAXT = 48
REACH = 2
ITERS = 2

TAU = 6.0
EPS = 1e-06
PRECISE = lax.Precision.HIGHEST

WEIGHT = 1.0 / (BR * MAXT)
SIGMA = math.exp(TAU) * WEIGHT
EXP2 = TAU / EMB * math.log2(math.e)
GROUP = 8
SHARDS = 6
F32 = jnp.float32
BF16 = jnp.bfloat16
VMEM = pl.BlockSpec(memory_space=pltpu.VMEM)
SMEM = pl.BlockSpec(memory_space=pltpu.SMEM)


def swapped(value, axis, bits):
    count = lax.axis_size(axis)
    return lax.ppermute(value, axis, [(i, i ^ bits) for i in range(count)])


def rotated(value, axis, steps):
    count = lax.axis_size(axis)
    return lax.ppermute(value, axis, [(i, (i + steps) % count) for i in range(count)])


def other_side(value):
    count = lax.axis_size("rows")
    chips = count // 2
    pairs = []
    for r in range(count):
        chip, core = divmod(r, 2)
        to = (chip + 1) % chips if chip % 2 else (chip - 1) % chips
        pairs.append((r, to * 2 + core))
    return lax.ppermute(value, "rows", pairs)


def after(value, *others):
    return lax.optimization_barrier((value, *others))[0]


def across(value):
    return swapped(value, "rows", 2), other_side(value), swapped(value, "rows", 1)


def by_core(side_a, side_b):
    return [side_a, swapped(side_a, "rows", 1), side_b, swapped(side_b, "rows", 1)]


def sum_tiles(value):
    return value + sum(rotated(value, "tiles", n) for n in range(1, lax.axis_size("tiles")))


def sum_rows(value):
    rows, bits = lax.axis_size("rows"), 2
    while bits < rows:
        span = min(4, rows // bits)
        value = value + sum(swapped(value, "rows", k * bits) for k in range(1, span))
        bits *= span
    return value


def sum_chips(value, part):
    rows, tiles = lax.axis_size("rows"), lax.axis_size("tiles")
    if rows // 2 != tiles or tiles != 4:
        total = (sum_tiles if part else sum_rows)(value)
        return total, total
    parts = [value]
    for step in range(1, 4):
        pairs = []
        for r in range(rows):
            for t in range(tiles):
                along_rows = r % 2 == part
                to = (r ^ (2 * step), t) if along_rows else (r, (t + step) % tiles)
                pairs.append((r * tiles + t, to[0] * tiles + to[1]))
        parts.append(lax.ppermute(value, ("rows", "tiles"), pairs))
    return sum(parts), parts[1]


def after_list(values, other):
    return [after(values[0], other), *values[1:]]


def dot_t(a, b):
    return lax.dot_general(a, b, (((1,), (1,)), ((), ())), preferred_element_type=F32)


def dot_exact(a, b):
    return lax.dot_general(
        a, b, (((1,), (1,)), ((), ())), precision=PRECISE, preferred_element_type=F32
    )


def unit_of(rows):
    values = rows.astype(F32)
    mean = jnp.sum(values * values, axis=1, keepdims=True) * (1.0 / EMB)
    return (values * lax.rsqrt(mean + EPS)).astype(BF16)


def pack_kernel(meta, emb, block, step, cols, emb_out, vec_out, cols_out, block_buf, step_buf, sems):
    here, width = meta[0], emb_out.shape[0]
    copies = [
        pltpu.make_async_copy(emb.at[pl.ds(here * width, width), :], emb_out, sems.at[0]),
        pltpu.make_async_copy(block, block_buf, sems.at[1]),
        pltpu.make_async_copy(step, step_buf, sems.at[2]),
    ]
    for copy in copies:
        copy.start()
    cols_out[...] = cols[...]
    copies[1].wait()
    vec_out[:K, :] = block_buf[...].astype(BF16)
    copies[2].wait()
    vec_out[K:, :] = step_buf[...].astype(BF16)
    copies[0].wait()


def group_copies(count, first, source, target, sems, body):
    @pl.loop(0, (count + GROUP - 1) // GROUP)
    def _(step):
        at = pl.ds(first + step * GROUP, GROUP)
        body(pltpu.make_async_copy(source.at[at], target.at[at], sems.at[step]))


def build_tiles(blocks, first, items, unit_own, unit_ext, tiles, stored=None, sems=None):
    count = items[items.shape[0] - 1]

    @pl.loop(0, (count + GROUP - 1) // GROUP)
    def _(step):
        picked = [items[step * GROUP + g] for g in range(GROUP)]
        scores = [dot_t(unit_ext[f // blocks], unit_own[f % blocks]) for f in picked]
        for g in range(GROUP):
            tiles[first + step * GROUP + g] = jnp.exp2(scores[g] * EXP2).astype(BF16)
        if stored is not None:
            at = pl.ds(first + step * GROUP, GROUP)
            pltpu.make_async_copy(tiles.at[at], stored.at[at], sems.at[step]).start()


def unit_kernel(emb, unit, buf, sems):
    blocks, parts = unit.shape[0], sems.shape[0]
    each = blocks // parts
    copies = [
        pltpu.make_async_copy(
            emb.at[pl.ds(n * each, each)], buf.at[pl.ds(n * each, each)], sems.at[n]
        )
        for n in range(parts)
    ]
    for copy in copies:
        copy.start()
    for n, copy in enumerate(copies):
        copy.wait()

        @pl.loop(n * each, (n + 1) * each)
        def _(b):
            unit[b] = unit_of(buf[b])


def near_kernel(
    blocks, share, meta, items, unit_own, emb_core, diag_out, stored, unit_ext, tiles, sems
):
    here = meta[0]
    for i in range(share):
        unit_ext[i] = unit_own[here * share + i]
        unit_ext[share + i] = unit_of(emb_core[pl.ds(i * BR, BR), :])
    rows = lax.broadcasted_iota(jnp.int32, (BR, BR), 0)
    cols = lax.broadcasted_iota(jnp.int32, (BR, BR), 1)
    for i in range(share):
        unit = unit_ext[i]
        weights = jnp.exp2(dot_t(unit, unit) * EXP2)
        on_diag = rows == cols
        diag_out[:, pl.ds(i * BR, BR)] = (
            jnp.sum(jnp.where(on_diag, weights, 0.0), axis=0, keepdims=True) * WEIGHT - SIGMA
        )
        tiles[i] = jnp.where(on_diag, 0.0, weights).astype(BF16)
    at = pl.ds(0, share)
    copy = pltpu.make_async_copy(tiles.at[at], stored.at[at], sems.at[sems.shape[0] - 1])
    copy.start()
    build_tiles(blocks, share, items, unit_own, unit_ext, tiles, stored, sems)
    count = items[items.shape[0] - 1]
    group_copies(count, share, tiles, stored, sems, lambda copy: copy.wait())
    copy.wait()


def apply_tiles(blocks, share, devices, here, items, tiles, vec, outs, vec_ext, acc):
    for j, ref in enumerate(vec):
        for i in range(share):
            vec_ext[j * share + i] = ref[:, pl.ds(i * BR, BR)]
    acc[...] = jnp.zeros_like(acc)
    for i in range(share):
        acc[here * share + i] = jnp.dot(vec_ext[i], tiles[0][i], preferred_element_type=F32)
    for part in range(2):
        count, first, base = items[part][items[part].shape[0] - 1], (share, 0)[part], (0, 2 * share)[part]

        @pl.loop(0, (count + GROUP - 1) // GROUP)
        def _(step):
            picked = []
            for g in range(GROUP):
                at = step * GROUP + g
                flat = items[part][at]
                picked.append(
                    (base + flat // blocks, jnp.where(at < count, flat % blocks, blocks))
                )
            parts = [
                jnp.dot(
                    vec_ext[ext],
                    tiles[part][first + step * GROUP + g],
                    preferred_element_type=F32,
                )
                for g, (ext, _) in enumerate(picked)
            ]
            for (_, to), value in zip(picked, parts):
                acc[to] += value

    for n, out in enumerate(outs):
        rows = pl.ds(n // devices * K, K)
        at_block = lax.rem(here + n % devices, devices) * share
        for i in range(share):
            value = acc[at_block + i, rows, :] * WEIGHT
            out[:, pl.ds(i * BR, BR)] = value.astype(out.dtype)


def far_kernel(blocks, share, devices, *refs):
    meta, items, stored, unit_own = refs[0], refs[1:3], refs[3], refs[4]
    emb, vec = refs[5 : 3 + SHARDS], refs[3 + SHARDS : 3 + 2 * SHARDS]
    outs, (near, far, unit_ext, vec_ext, acc, sems) = refs[3 + 2 * SHARDS : -6], refs[-6:]
    count, at = items[0][items[0].shape[0] - 1], pl.ds(0, share)
    copy = pltpu.make_async_copy(stored.at[at], near.at[at], sems.at[sems.shape[0] - 1])
    copy.start()
    group_copies(count, share, stored, near, sems, lambda copy: copy.start())
    for j, ref in enumerate(emb):
        for i in range(share):
            unit_ext[j * share + i] = unit_of(ref[pl.ds(i * BR, BR), :])
    build_tiles(blocks, 0, items[1], unit_own, unit_ext, far)
    copy.wait()
    group_copies(count, share, stored, near, sems, lambda copy: copy.wait())
    apply_tiles(blocks, share, devices, meta[0], items, (near, far), vec, outs, vec_ext, acc)


def apply_kernel(blocks, share, devices, *refs):
    meta, items, tiles = refs[0], refs[1:3], refs[3:5]
    vec, outs, (vec_ext, acc) = refs[5 : 5 + SHARDS], refs[5 + SHARDS : -2], refs[-2:]
    apply_tiles(blocks, share, devices, meta[0], items, tiles, vec, outs, vec_ext, acc)


def summed(parts, diag, vectors):
    value = parts[0][...] + diag[...] * vectors
    for ref in parts[1:]:
        value = value + ref[...].astype(F32)
    return value


def image_kernel(devices, *refs):
    parts, (diag, vec, out, out_half) = refs[:devices], refs[devices:]
    value = summed(parts, diag, vec[...])
    out[...] = value
    out_half[...] = value.astype(BF16)


def mul(a, b):
    return jnp.dot(a, b, precision=PRECISE, preferred_element_type=F32)


def eye_mask(n):
    shape = (n, n)
    return lax.broadcasted_iota(jnp.int32, shape, 0) == lax.broadcasted_iota(jnp.int32, shape, 1)


def as_row(column):
    return jnp.sum(jnp.where(eye_mask(K), column, 0.0), axis=0, keepdims=True)


def step_coefficients(g_vv, g_vs, g_ss, g_jv, g_js, g_jj, rotation, total):
    m_t = g_jv * (1.0 / total) + SIGMA * (g_vv * (1.0 / total) - eye_mask(K).astype(F32))
    resid_sq = (
        jnp.sum(jnp.where(eye_mask(K), g_jj, 0.0), axis=1, keepdims=True)
        - 2.0 * jnp.sum(m_t * g_jv, axis=1, keepdims=True)
        + jnp.sum(m_t * mul(m_t, g_vv), axis=1, keepdims=True)
    )
    resid_inv = 1.0 / jnp.sqrt(jnp.maximum(resid_sq, 0.0) * (1.0 / total) + EPS)
    on_v, on_resid, on_s = rotation[:K].T, rotation[K : 2 * K].T, rotation[2 * K :].T
    p_j = on_resid * as_row(resid_inv)
    p_step = -mul(p_j, m_t)
    coef = jnp.concatenate(
        [
            jnp.concatenate([on_v + p_step, on_s, p_j], axis=1),
            jnp.concatenate([p_step, on_s, p_j], axis=1),
        ],
        axis=0,
    )
    gram = jnp.concatenate(
        [
            jnp.concatenate([g_vv, g_vs, g_jv.T], axis=1),
            jnp.concatenate([g_vs.T, g_ss, g_js.T], axis=1),
            jnp.concatenate([g_jv, g_js, g_jj], axis=1),
        ],
        axis=0,
    )
    on_gram = mul(coef, gram)
    comb_sq = jnp.sum(on_gram[:K] * coef[:K], axis=1, keepdims=True)
    scale = 1.0 / jnp.sqrt(jnp.maximum(comb_sq, 0.0) * (1.0 / total) + EPS)
    return coef, on_gram, jnp.concatenate([scale, scale], axis=0)


def gram_kernel(devices, meta, x_ref, y_ref, j_ref, diag, *refs):
    parts, (rows, keep, send) = refs[:devices], refs[devices:]
    rows[:K, :] = x_ref[...]
    rows[K : 2 * K, :] = y_ref[...]
    rows[2 * K : 3 * K, :] = j_ref[...]
    rows[3 * K :, :] = summed(parts, diag, y_ref[...])
    g = dot_exact(rows[...], rows[...])
    packed = jnp.concatenate(
        [
            g[:K, : 2 * K],
            jnp.concatenate([g[K : 2 * K, K : 2 * K], g[3 * K :, 3 * K :]], axis=1),
            g[: 3 * K, 2 * K :],
        ],
        axis=0,
    )
    half = keep.shape[0]
    keep[...] = jnp.where(meta[1] == 0, packed[:half], packed[half:])
    send[...] = jnp.where(meta[1] == 0, packed[half:], packed[:half])


def first_kernel(total, meta, rot_ref, rows, mine, other, new_out, part_out, coef_out, g_out, l_out):
    packed = jnp.concatenate(
        [
            jnp.where(meta[1] == 0, mine[...], other[...]),
            jnp.where(meta[1] == 0, other[...], mine[...]),
        ],
        axis=0,
    )
    xx, xy = packed[:K, :K], packed[:K, K:]
    yy, tt = packed[K : 2 * K, :K], packed[K : 2 * K, K:]
    xj, xt = packed[2 * K : 3 * K, :K], packed[2 * K : 3 * K, K:]
    yj, yt = packed[3 * K : 4 * K, :K], packed[3 * K : 4 * K, K:]
    jj, jt = packed[4 * K :, :K], packed[4 * K :, K:]

    def inv_rms(square):
        picked = jnp.sum(jnp.where(eye_mask(K), square, 0.0), axis=1, keepdims=True)
        return 1.0 / jnp.sqrt(picked * (1.0 / total) + EPS)

    x_col, y_col = inv_rms(xx), inv_rms(yy)
    x_row, y_row = as_row(x_col), as_row(y_col)
    coef, on_gram, scale = step_coefficients(
        xx * x_col * x_row,
        xy * x_col * y_row,
        yy * y_col * y_row,
        xj.T * x_col * x_row,
        yj.T * x_col * y_row,
        jj * x_col * x_row,
        rot_ref[...],
        total,
    )
    coef = scale * coef
    g_out[...] = dot_exact(scale * on_gram, coef)
    coef = coef * jnp.concatenate([x_row, y_row, x_row], axis=1)
    coef_out[...] = coef
    new_out[...] = mul(coef, rows[: 3 * K, :])
    known = coef[:K, : 2 * K]
    part_out[...] = mul(known, rows[2 * K :, :])
    j_t = jnp.concatenate(
        [
            jnp.concatenate([xj.T, yj.T, jj, jt], axis=1),
            jnp.concatenate([xt.T, yt.T, jt.T, tt], axis=1),
        ],
        axis=0,
    )
    l_out[...] = mul(known, j_t)


def twice_kernel(devices, rows, diag, *refs):
    parts, (q_out, out) = refs[:devices], refs[devices:]
    q = summed(parts, diag, rows[2 * K : 3 * K, :])
    q_out[...] = q
    g = dot_exact(q, rows[...])
    out[:K, :] = g[:, : 2 * K]
    out[K : 2 * K, :] = g[:, 2 * K :]
    qq = dot_exact(q, q)
    out[2 * K :, :K] = qq[: K // 2]
    out[2 * K :, K:] = qq[K // 2 :]


def image_again_kernel(part, coef, q, out):
    out[...] = part[...] + mul(coef[:K, 2 * K :], q[...])


def last_kernel(total, rot_ref, new, j_ref, coef_ref, g_ref, l_ref, h_ref, v_out, s_out):
    coef, gram = coef_ref[...], g_ref[...]
    q_xy, q_jt = h_ref[:K, :], h_ref[K : 2 * K, :]
    qq = jnp.concatenate([h_ref[2 * K :, :K], h_ref[2 * K :, K:]], axis=0)
    q_all = jnp.concatenate([q_xy, q_jt, qq], axis=1)
    image = mul(coef[:K, 2 * K :], q_all)
    on_rows = l_ref[...] + image[:, : 4 * K]
    on_q = dot_exact(coef[:K, : 2 * K], q_jt) + image[:, 4 * K :]
    j_new = dot_exact(on_rows[:, : 3 * K], coef)
    g_jj = dot_exact(jnp.concatenate([on_rows[:, 2 * K :], on_q], axis=1), coef[:K])
    coef, _, scale = step_coefficients(
        gram[:K, :K],
        gram[:K, K:],
        gram[K:, K:],
        j_new[:, :K],
        j_new[:, K:],
        g_jj,
        rot_ref[...],
        total,
    )
    both = scale * mul(coef, jnp.concatenate([new[...], j_ref[...]], axis=0))
    v_out[...], s_out[...] = both[:K], both[K:]


def call(kernel, outs, *args, smem=0, hbm=0, scratch=(), us=0.0):
    any_memory = pl.BlockSpec(memory_space=pl.ANY)
    args = [
        pltpu.with_memory_space_constraint(arg, pltpu.HBM) if smem <= n < smem + hbm else arg
        for n, arg in enumerate(args)
    ]
    return pl.pallas_call(
        kernel,
        out_shape=tuple(
            pltpu.HBM(*out[:2]) if len(out) > 2 else jax.ShapeDtypeStruct(*out) for out in outs
        ),
        in_specs=[SMEM] * smem + [any_memory] * hbm + [VMEM] * (len(args) - smem - hbm),
        out_specs=tuple(any_memory if len(out) > 2 else VMEM for out in outs),
        scratch_shapes=list(scratch),
        compiler_params=pltpu.CompilerParams(vmem_limit_bytes=16 * 1024 * 1024),
        cost_estimate=pl.CostEstimate(
            flops=int(us * 1e9), bytes_accessed=0, transcendentals=0
        ),
    )(*args)


def tile_list(cols, counts, here, row, share, devices):
    blocks, span = cols.shape[0], cols.shape[1] // devices
    slot = jnp.concatenate(
        [
            (here ^ n) * span + lax.broadcasted_iota(jnp.int32, (blocks, span), 1)
            for n in range(devices)
        ],
        axis=1,
    )
    col = cols
    block = row * blocks + lax.broadcasted_iota(jnp.int32, col.shape, 0)
    shard, inner = col // blocks, col % blocks
    other_core = (shard % 2 != row % 2).astype(jnp.int32)
    chip, own_chip = shard // 2, row // 2
    place = other_core + jnp.where(chip == own_chip, 0, jnp.where(chip == own_chip ^ 1, 2, 4))
    mine = (slot < counts[:, None]) & (inner // share == here) & (col != block)
    ext = jnp.where(mine, place * share + inner % share, -1)
    wanted = lax.broadcasted_iota(jnp.int32, (SHARDS * share, blocks, 1), 0)
    mask = jnp.any(ext[None] == wanted, axis=2).astype(F32)
    lists = []
    for part in (mask[: 2 * share], mask[2 * share :]):
        flat = part.size
        part = part.reshape(flat)
        index = jnp.arange(flat, dtype=jnp.int32)
        upto = (index[:, None] <= index[None, :]).astype(F32)
        place = jnp.dot(part, upto).astype(jnp.int32)
        wide = jnp.arange(flat + GROUP + 1, dtype=jnp.int32)[None, :]
        used = part[:, None] > 0
        hit = (place[:, None] == wide + 1) & used
        last = (wide == flat + GROUP) & used
        lists.append(jnp.sum(jnp.where(hit, index[:, None], last.astype(jnp.int32)), axis=0))
    return lists


def local(embedding, start_block, start_step, rotations, neighbour_cols, tile_counts):
    devices = lax.axis_size("tiles")
    width = start_block.shape[1]
    share = width // BR
    blocks = tile_counts.shape[0]
    total = width * devices * lax.axis_size("rows")
    here, row = lax.axis_index("tiles"), lax.axis_index("rows")

    meta = jnp.stack([here, row % 2])
    own_emb, own_vec, cols = call(
        pack_kernel,
        [((width, EMB), BF16), ((2 * K, width), BF16), (neighbour_cols.shape, jnp.int32)],
        meta,
        embedding,
        start_block,
        start_step,
        neighbour_cols,
        smem=1,
        hbm=3,
        scratch=[
            pltpu.VMEM((K, width), F32),
            pltpu.VMEM((K, width), F32),
            pltpu.SemaphoreType.DMA((3,)),
        ],
        us=1.0,
    )
    emb_a, emb_b, emb_core = across(own_emb)
    lists = after(cols, emb_core)
    bits = 1
    while bits < devices:
        lists = jnp.concatenate([lists, swapped(lists, "tiles", bits)], axis=1)
        bits *= 2
    items = tile_list(lists, tile_counts, here, row, share, devices)
    own_vec = after(own_vec, emb_core)
    vec_a, vec_b, vec_core = across(own_vec)
    (unit_own,) = call(
        unit_kernel,
        [((blocks, BR, EMB), BF16)],
        after(embedding.reshape(blocks, BR, EMB), emb_core),
        hbm=1,
        scratch=[pltpu.VMEM((blocks, BR, EMB), BF16), pltpu.SemaphoreType.DMA((4,))],
        us=2.6,
    )
    near, far = 2 * share * blocks, (SHARDS - 2) * share * blocks
    near_shape, far_shape = (share + near + GROUP, BR, BR), (far + GROUP, BR, BR)
    near_sems = pltpu.SemaphoreType.DMA((near // GROUP + 2,))
    diag, tiles_near = call(
        functools.partial(near_kernel, blocks, share),
        [((1, width), F32), (near_shape, BF16, "hbm")],
        meta,
        items[0],
        unit_own,
        emb_core,
        smem=2,
        scratch=[
            pltpu.VMEM((2 * share, BR, EMB), BF16),
            pltpu.VMEM(near_shape, BF16),
            near_sems,
        ],
        us=2.0,
    )
    emb_a, emb_b, vec_a, vec_b = (after(side, diag) for side in (emb_a, emb_b, vec_a, vec_b))
    parts = call(
        functools.partial(far_kernel, blocks, share, devices),
        ([((K, width), F32)] + [((K, width), BF16)] * (devices - 1)) * 2
        + [(near_shape, BF16), (far_shape, BF16)],
        meta,
        *items,
        tiles_near,
        unit_own,
        *by_core(emb_a, emb_b),
        own_vec,
        vec_core,
        *by_core(vec_a, vec_b),
        smem=3,
        hbm=1,
        scratch=[
            pltpu.VMEM(((SHARDS - 2) * share, BR, EMB), BF16),
            pltpu.VMEM((SHARDS * share, 2 * K, BR), BF16),
            pltpu.VMEM((blocks + 1, 2 * K, BR), F32),
            near_sems,
        ],
        us=5.0,
    )
    parts, tiles_near, tiles_far = parts[:-2], parts[-2], parts[-1]

    def applied(halo):
        return call(
            functools.partial(apply_kernel, blocks, share, devices),
            [((K, width), F32)] + [((K, width), BF16)] * (devices - 1),
            meta,
            *items,
            tiles_near,
            tiles_far,
            *halo,
            smem=3,
            scratch=[
                pltpu.VMEM((SHARDS * share, K, BR), BF16),
                pltpu.VMEM((blocks + 1, K, BR), F32),
            ],
            us=3.0,
        )

    def gathered(parts):
        return [parts[0]] + [rotated(part, "tiles", n + 1) for n, part in enumerate(parts[1:])]

    parts, step_parts = gathered(parts[:devices]), gathered(parts[devices:])
    image, image_half = call(
        functools.partial(image_kernel, devices),
        [((K, width), F32), ((K, width), BF16)],
        *after_list(parts, step_parts[1]),
        diag,
        start_block,
        us=0.1,
    )
    image_a, image_b, image_core = across(image_half)
    half = 5 * K // 2
    rows, keep, send = call(
        functools.partial(gram_kernel, devices),
        [((4 * K, width), F32)] + [((half, 2 * K), F32)] * 2,
        meta,
        start_block,
        start_step,
        after(image, image_core),
        diag,
        *step_parts,
        smem=1,
        us=1.0,
    )
    image_vec = [image_half, image_core, *by_core(after(image_a, keep), after(image_b, keep))]
    gram = keep + swapped(send, "rows", 1)
    parts = gathered(applied(image_vec))
    gram = sum_rows(after(gram, parts[1]))
    twice, products = call(
        functools.partial(twice_kernel, devices),
        [((K, width), F32), ((half, 2 * K), F32)],
        rows,
        diag,
        *parts,
        us=0.8,
    )
    products = products + swapped(products, "rows", 1)
    gram = sum_tiles(after(gram, products))
    products, _ = sum_chips(products, 0)
    products, _ = sum_chips(products, 1)
    new, part, coef, gram, known = call(
        functools.partial(first_kernel, total),
        [
            ((2 * K, width), F32),
            ((K, width), F32),
            ((2 * K, 3 * K), F32),
            ((2 * K, 2 * K), F32),
            ((K, 4 * K), F32),
        ],
        meta,
        rotations[0],
        rows,
        gram,
        swapped(gram, "rows", 1),
        smem=1,
        us=0.0,
    )
    (image,) = call(image_again_kernel, [((K, width), F32)], part, coef, twice, us=0.0)
    return call(
        functools.partial(last_kernel, total),
        [((K, width), F32)] * 2,
        rotations[1],
        new,
        image,
        coef,
        gram,
        known,
        products,
        us=2.5,
    )


def solution(mesh):
    return jax.shard_map(
        local,
        mesh=mesh,
        in_specs=(
            P("rows", None),
            P(None, ("rows", "tiles")),
            P(None, ("rows", "tiles")),
            P(),
            P("rows", "tiles"),
            P("rows"),
        ),
        out_specs=(P(None, ("rows", "tiles")), P(None, ("rows", "tiles"))),
        check_vma=False,
    )
```

```python
import functools
import math

import jax
import jax.numpy as jnp
from jax import lax
from jax.experimental import pallas as pl
from jax.experimental.pallas import tpu as pltpu
from jax.sharding import PartitionSpec as P

EMB = 256
K = 64
BR = 128
MAXT = 48
REACH = 2
ITERS = 2

TAU = 6.0
EPS = 1e-06
PRECISE = lax.Precision.HIGHEST

WEIGHT = 1.0 / (BR * MAXT)
SIGMA = math.exp(TAU) * WEIGHT
EXP2 = TAU / EMB * math.log2(math.e)
GROUP = 16
SHARDS = 6
F32 = jnp.float32
BF16 = jnp.bfloat16
VMEM = pl.BlockSpec(memory_space=pltpu.VMEM)
SMEM = pl.BlockSpec(memory_space=pltpu.SMEM)


def swapped(value, axis, bits):
    count = lax.axis_size(axis)
    return lax.ppermute(value, axis, [(i, i ^ bits) for i in range(count)])


def rotated(value, axis, steps):
    count = lax.axis_size(axis)
    return lax.ppermute(value, axis, [(i, (i + steps) % count) for i in range(count)])


def other_side(value, core_0_too=True):
    count = lax.axis_size("rows")
    chips = count // 2
    pairs = []
    for r in range(count):
        chip, core = divmod(r, 2)
        to = (chip + 1) % chips if chip % 2 else (chip - 1) % chips
        pairs.append((r, to * 2 + core if core or core_0_too else r ^ 2))
    return lax.ppermute(value, "rows", pairs)


def after(value, *others):
    return lax.optimization_barrier((value, *others))[0]


def across(value):
    return swapped(value, "rows", 2), other_side(value), swapped(value, "rows", 1)


def by_core(side_a, side_b):
    return [side_a, swapped(side_a, "rows", 1), side_b, swapped(side_b, "rows", 1)]


def sum_along(value, axis, bits):
    while bits < lax.axis_size(axis):
        value = value + swapped(value, axis, bits)
        bits *= 2
    return value


def sum_chips(value, part):
    rows, tiles = lax.axis_size("rows"), lax.axis_size("tiles")
    if rows // 2 != tiles or tiles != 4:
        return sum_along(value, "tiles", 1) if part else sum_along(value, "rows", 2)
    parts = [value]
    for step in range(1, 4):
        pairs = []
        for r in range(rows):
            for t in range(tiles):
                along_rows = r % 2 == part
                to = (r ^ (2 * step), t) if along_rows else (r, (t + step) % tiles)
                pairs.append((r * tiles + t, to[0] * tiles + to[1]))
        parts.append(lax.ppermute(value, ("rows", "tiles"), pairs))
    return sum(parts)


def dot_t(a, b):
    return lax.dot_general(a, b, (((1,), (1,)), ((), ())), preferred_element_type=F32)


def dot_exact(a, b):
    return lax.dot_general(
        a, b, (((1,), (1,)), ((), ())), precision=PRECISE, preferred_element_type=F32
    )


def unit_of(rows):
    values = rows.astype(F32)
    mean = jnp.sum(values * values, axis=1, keepdims=True) * (1.0 / EMB)
    return (values * lax.rsqrt(mean + EPS)).astype(BF16)


def pack_kernel(meta, emb, block, step, emb_out, vec_out, block_buf, step_buf, sems):
    here, width = meta[0], emb_out.shape[0]
    copies = [
        pltpu.make_async_copy(emb.at[pl.ds(here * width, width), :], emb_out, sems.at[0]),
        pltpu.make_async_copy(block, block_buf, sems.at[1]),
        pltpu.make_async_copy(step, step_buf, sems.at[2]),
    ]
    for copy in copies:
        copy.start()
    copies[1].wait()
    vec_out[:K, :] = block_buf[...].astype(BF16)
    copies[2].wait()
    vec_out[K:, :] = step_buf[...].astype(BF16)
    copies[0].wait()


def group_copies(count, first, source, target, sems, body):
    @pl.loop(0, (count + GROUP - 1) // GROUP)
    def _(step):
        at = pl.ds(first + step * GROUP, GROUP)
        body(pltpu.make_async_copy(source.at[at], target.at[at], sems.at[step]))


def build_tiles(blocks, first, items, unit_own, unit_ext, tiles, stored=None, sems=None):
    count = items[items.shape[0] - 1]

    @pl.loop(0, (count + GROUP - 1) // GROUP)
    def _(step):
        picked = [items[step * GROUP + g] for g in range(GROUP)]
        scores = [dot_t(unit_ext[f // blocks], unit_own[f % blocks]) for f in picked]
        for g in range(GROUP):
            tiles[first + step * GROUP + g] = jnp.exp2(scores[g] * EXP2).astype(BF16)
        if stored is not None:
            at = pl.ds(first + step * GROUP, GROUP)
            pltpu.make_async_copy(tiles.at[at], stored.at[at], sems.at[step]).start()


def unit_kernel(emb, unit, buf, sems):
    blocks, parts = unit.shape[0], sems.shape[0]
    each = blocks // parts
    copies = [
        pltpu.make_async_copy(
            emb.at[pl.ds(n * each, each)], buf.at[pl.ds(n * each, each)], sems.at[n]
        )
        for n in range(parts)
    ]
    for copy in copies:
        copy.start()
    for n, copy in enumerate(copies):
        copy.wait()

        @pl.loop(n * each, (n + 1) * each)
        def _(b):
            unit[b] = unit_of(buf[b])


def near_kernel(
    blocks, share, meta, items, unit_own, emb_core, diag_out, stored, unit_ext, tiles, sems
):
    here = meta[0]
    for i in range(share):
        unit_ext[i] = unit_own[here * share + i]
        unit_ext[share + i] = unit_of(emb_core[pl.ds(i * BR, BR), :])
    rows = lax.broadcasted_iota(jnp.int32, (BR, BR), 0)
    cols = lax.broadcasted_iota(jnp.int32, (BR, BR), 1)
    for i in range(share):
        unit = unit_ext[i]
        weights = jnp.exp2(dot_t(unit, unit) * EXP2)
        on_diag = rows == cols
        diag_out[:, pl.ds(i * BR, BR)] = (
            jnp.sum(jnp.where(on_diag, weights, 0.0), axis=0, keepdims=True) * WEIGHT - SIGMA
        )
        tiles[i] = jnp.where(on_diag, 0.0, weights).astype(BF16)
    at = pl.ds(0, share)
    copy = pltpu.make_async_copy(tiles.at[at], stored.at[at], sems.at[sems.shape[0] - 1])
    copy.start()
    build_tiles(blocks, share, items, unit_own, unit_ext, tiles, stored, sems)
    count = items[items.shape[0] - 1]
    group_copies(count, share, tiles, stored, sems, lambda copy: copy.wait())
    copy.wait()


def apply_tiles(blocks, share, devices, here, items, tiles, outs, vec_ext, acc):
    acc[...] = jnp.zeros_like(acc)
    for i in range(share):
        acc[here * share + i] = jnp.dot(vec_ext[i], tiles[0][i], preferred_element_type=F32)
    for part in range(2):
        count, first, base = items[part][items[part].shape[0] - 1], (share, 0)[part], (0, 2 * share)[part]

        @pl.loop(0, (count + GROUP - 1) // GROUP)
        def _(step):
            picked = []
            for g in range(GROUP):
                at = step * GROUP + g
                flat = items[part][at]
                picked.append(
                    (base + flat // blocks, jnp.where(at < count, flat % blocks, blocks))
                )
            parts = [
                jnp.dot(
                    vec_ext[ext],
                    tiles[part][first + step * GROUP + g],
                    preferred_element_type=F32,
                )
                for g, (ext, _) in enumerate(picked)
            ]
            for (_, to), value in zip(picked, parts):
                acc[to] += value

    for n, out in enumerate(outs):
        rows = pl.ds(n // devices * K, K)
        at_block = lax.rem(here + n % devices, devices) * share
        for i in range(share):
            value = acc[at_block + i, rows, :] * WEIGHT
            out[:, pl.ds(i * BR, BR)] = value.astype(out.dtype)


def far_kernel(blocks, share, devices, *refs):
    meta, items, stored, unit_own = refs[0], refs[1:3], refs[3], refs[4]
    emb, vec = refs[5 : 3 + SHARDS], refs[3 + SHARDS : 3 + 2 * SHARDS]
    outs, (near, far, unit_ext, vec_ext, acc, sems) = refs[3 + 2 * SHARDS : -6], refs[-6:]
    count, at = items[0][items[0].shape[0] - 1], pl.ds(0, share)
    copy = pltpu.make_async_copy(stored.at[at], near.at[at], sems.at[sems.shape[0] - 1])
    copy.start()
    group_copies(count, share, stored, near, sems, lambda copy: copy.start())
    for j, ref in enumerate(emb):
        for i in range(share):
            unit_ext[j * share + i] = unit_of(ref[pl.ds(i * BR, BR), :])
    build_tiles(blocks, 0, items[1], unit_own, unit_ext, far)
    copy.wait()
    group_copies(count, share, stored, near, sems, lambda copy: copy.wait())
    for j, ref in enumerate(vec):
        for i in range(share):
            vec_ext[j * share + i] = ref[:, pl.ds(i * BR, BR)]
    apply_tiles(blocks, share, devices, meta[0], items, (near, far), outs, vec_ext, acc)


def apply_kernel(blocks, share, devices, *refs):
    meta, items, tiles = refs[0], refs[1:3], refs[3:5]
    own, core, mine, other = refs[5:9]
    outs, (vec_ext, acc) = refs[9:-2], refs[-2:]
    odd = meta[1]
    slots = [(own, 0, 0), (core, 0, 1)]
    slots += [(mine, 0, 2 + 2 * odd), (mine, 1, 3 + 2 * odd)]
    slots += [(other, 0, 5 - 2 * odd), (other, 1, 4 - 2 * odd)]
    for ref, half, slot in slots:
        for i in range(share):
            vec_ext[slot * share + i] = ref[pl.ds(half * K, K), pl.ds(i * BR, BR)]
    apply_tiles(blocks, share, devices, meta[0], items, tiles, outs, vec_ext, acc)


def summed(parts, diag, vectors):
    value = parts[0][...] + diag[...] * vectors
    for ref in parts[1:]:
        value = value + ref[...].astype(F32)
    return value


def image_kernel(devices, *refs):
    parts, (diag, vec, out, out_half) = refs[:devices], refs[devices:]
    value = summed(parts, diag, vec[...])
    out[...] = value
    out_half[...] = value.astype(BF16)


def mul(a, b):
    return jnp.dot(a, b, precision=PRECISE, preferred_element_type=F32)


def halves_of(value):
    high = value.astype(BF16)
    return high, (value - high.astype(F32)).astype(BF16)


def mul3(a, b):
    (a_high, a_low), (b_high, b_low) = halves_of(a), halves_of(b)
    return jnp.dot(
        jnp.concatenate([a_high, a_high, a_low], axis=1),
        jnp.concatenate([b_high, b_low, b_high], axis=0),
        preferred_element_type=F32,
    )


def dot3(a, b):
    (a_high, a_low), (b_high, b_low) = halves_of(a), halves_of(b)
    return dot_t(
        jnp.concatenate([a_high, a_high, a_low], axis=1),
        jnp.concatenate([b_high, b_low, b_high], axis=1),
    )


def eye_mask(n):
    shape = (n, n)
    return lax.broadcasted_iota(jnp.int32, shape, 0) == lax.broadcasted_iota(jnp.int32, shape, 1)


def as_row(column):
    return jnp.sum(jnp.where(eye_mask(K), column, 0.0), axis=0, keepdims=True)


def step_coefficients(g_vv, g_vs, g_ss, g_jv, g_js, g_jj, rotation, total):
    m_t = g_jv * (1.0 / total) + SIGMA * (g_vv * (1.0 / total) - eye_mask(K).astype(F32))
    resid_sq = jnp.sum(
        jnp.where(eye_mask(K), g_jj, 0.0) + m_t * (mul(m_t, g_vv) - 2.0 * g_jv),
        axis=1,
        keepdims=True,
    )
    resid_inv = 1.0 / jnp.sqrt(jnp.maximum(resid_sq, 0.0) * (1.0 / total) + EPS)
    on_v, on_resid, on_s = rotation[:, :K], rotation[:, K : 2 * K], rotation[:, 2 * K :]
    p_j = on_resid * as_row(resid_inv)
    p_step = -mul3(p_j, m_t)
    coef = jnp.concatenate(
        [
            jnp.concatenate([on_v + p_step, on_s, p_j], axis=1),
            jnp.concatenate([p_step, on_s, p_j], axis=1),
        ],
        axis=0,
    )
    gram = jnp.concatenate(
        [
            jnp.concatenate([g_vv, g_vs, g_jv.T], axis=1),
            jnp.concatenate([g_vs.T, g_ss, g_js.T], axis=1),
            jnp.concatenate([g_jv, g_js, g_jj], axis=1),
        ],
        axis=0,
    )
    on_gram = mul3(coef, gram)
    comb_sq = jnp.sum(on_gram[:K] * coef[:K], axis=1, keepdims=True)
    scale = 1.0 / jnp.sqrt(jnp.maximum(comb_sq, 0.0) * (1.0 / total) + EPS)
    return coef, on_gram, jnp.concatenate([scale, scale], axis=0)


def split_by_core(core, value, keep, send):
    half = keep.shape[0]
    keep[...] = jnp.where(core == 0, value[:half], value[half:])
    send[...] = jnp.where(core == 0, value[half:], value[:half])


def joined(core, mine, other):
    return jnp.concatenate(
        [
            jnp.where(core == 0, mine[...], other[...]),
            jnp.where(core == 0, other[...], mine[...]),
        ],
        axis=0,
    )


def gram_kernel(x_ref, y_ref, j_ref, rows, out):
    rows[:K, :] = x_ref[...]
    rows[K : 2 * K, :] = y_ref[...]
    rows[2 * K :, :] = j_ref[...]
    g = dot_exact(rows[...], rows[...])
    out[:K, :] = g[:K, : 2 * K]
    out[K : 2 * K, :K] = g[K : 2 * K, K : 2 * K]
    out[K : 2 * K, K:] = g[2 * K :, 2 * K :]
    out[2 * K :, :] = g[2 * K :, : 2 * K]


def first_step(packed, rotation, total):
    xx, xy = packed[:K, :K], packed[:K, K:]
    yy, jj = packed[K : 2 * K, :K], packed[K : 2 * K, K:]
    jx, jy = packed[2 * K :, :K], packed[2 * K :, K:]

    def inv_rms(square):
        picked = jnp.sum(jnp.where(eye_mask(K), square, 0.0), axis=1, keepdims=True)
        return 1.0 / jnp.sqrt(picked * (1.0 / total) + EPS)

    x_col, y_col = inv_rms(xx), inv_rms(yy)
    x_row, y_row = as_row(x_col), as_row(y_col)
    coef, on_gram, scale = step_coefficients(
        xx * x_col * x_row,
        xy * x_col * y_row,
        yy * y_col * y_row,
        jx * x_col * x_row,
        jy * x_col * y_row,
        jj * x_col * x_row,
        rotation,
        total,
    )
    coef = scale * coef
    gram = dot3(scale * on_gram, coef)
    coef = coef * jnp.concatenate([x_row, y_row, x_row], axis=1)
    return coef, gram, mul3(coef[:K, :K], jnp.concatenate([jx, jy, jj], axis=1))


def twice_kernel(devices, meta, rows, gram, step, diag, *refs):
    t_parts, q_parts = refs[:devices], refs[devices : 2 * devices]
    t_out, q_out, keep, send = refs[2 * devices :]
    t = summed(t_parts, diag, step[...])
    q = summed(q_parts, diag, rows[2 * K :, :])
    t_out[...] = t
    q_out[...] = q
    both = jnp.concatenate([t, q], axis=0)
    on_rows = dot3(both, rows[...])
    on_both = dot3(both, both)
    half = K // 2
    packed = jnp.concatenate(
        [
            gram[...],
            on_rows[:, : 2 * K],
            jnp.concatenate([on_rows[:K, 2 * K :], on_rows[K:, 2 * K :]], axis=1),
            on_both[K:],
            jnp.concatenate([on_both[:half, :K], on_both[half:K, :K]], axis=1),
        ],
        axis=0,
    )
    split_by_core(meta[1], packed, keep, send)


def last_kernel(total, meta, rot_ref, rows, t_ref, q_ref, mine, other, v_out, s_out):
    packed = joined(meta[1], mine, other)
    coef, gram, known = first_step(packed[: 3 * K], rot_ref[0], total)
    packed = packed[3 * K :]
    on_xy, on_j, on_both = packed[: 2 * K], packed[2 * K : 3 * K], packed[3 * K :]
    tq_j = jnp.concatenate([on_j[:, :K], on_j[:, K:]], axis=0)
    qt, qq = on_both[:K, :K], on_both[:K, K:]
    tt = jnp.concatenate([on_both[K:, :K], on_both[K:, K:]], axis=0)
    on_tq = jnp.concatenate(
        [jnp.concatenate([tt, qt.T], axis=1), jnp.concatenate([qt, qq], axis=1)], axis=0
    )
    image = mul3(coef[:K, K:], jnp.concatenate([on_xy, tq_j, on_tq], axis=1))
    on_rows = known + image[:, : 3 * K]
    on_tq = dot3(coef[:K, :K], tq_j) + image[:, 3 * K :]
    j_new = dot3(on_rows, coef)
    g_jj = dot3(jnp.concatenate([on_rows[:, 2 * K :], on_tq], axis=1), coef[:K])
    again, _, scale = step_coefficients(
        gram[:K, :K],
        gram[:K, K:],
        gram[K:, K:],
        j_new[:, :K],
        j_new[:, K:],
        g_jj,
        rot_ref[1],
        total,
    )
    on_new = mul3(again[:, : 2 * K], coef)
    on_image = mul3(again[:, 2 * K :], coef[:K])
    both = jnp.concatenate(
        [
            on_new[:, : 2 * K],
            on_new[:, 2 * K :] + on_image[:, :K],
            on_image[:, K:],
        ],
        axis=1,
    )
    both = scale * mul3(both, jnp.concatenate([rows[...], t_ref[...], q_ref[...]], axis=0))
    v_out[...], s_out[...] = both[:K], both[K:]


def call(kernel, outs, *args, smem=0, hbm=0, scratch=(), us=0.0):
    any_memory = pl.BlockSpec(memory_space=pl.ANY)
    args = [
        pltpu.with_memory_space_constraint(arg, pltpu.HBM) if smem <= n < smem + hbm else arg
        for n, arg in enumerate(args)
    ]
    return pl.pallas_call(
        kernel,
        out_shape=tuple(
            pltpu.HBM(*out[:2]) if len(out) > 2 else jax.ShapeDtypeStruct(*out) for out in outs
        ),
        in_specs=[SMEM] * smem + [any_memory] * hbm + [VMEM] * (len(args) - smem - hbm),
        out_specs=tuple(any_memory if len(out) > 2 else VMEM for out in outs),
        scratch_shapes=list(scratch),
        compiler_params=pltpu.CompilerParams(vmem_limit_bytes=16 * 1024 * 1024),
        cost_estimate=pl.CostEstimate(
            flops=int(us * 1e9), bytes_accessed=0, transcendentals=0
        ),
    )(*args)


def tile_list(cols, counts, here, row, share, devices):
    blocks, span = cols.shape[0], cols.shape[1] // devices
    slot = jnp.concatenate(
        [
            (here ^ n) * span + lax.broadcasted_iota(jnp.int32, (blocks, span), 1)
            for n in range(devices)
        ],
        axis=1,
    )
    col = cols
    block = row * blocks + lax.broadcasted_iota(jnp.int32, col.shape, 0)
    shard, inner = col // blocks, col % blocks
    other_core = (shard % 2 != row % 2).astype(jnp.int32)
    chip, own_chip = shard // 2, row // 2
    place = other_core + jnp.where(chip == own_chip, 0, jnp.where(chip == own_chip ^ 1, 2, 4))
    mine = (slot < counts[:, None]) & (inner // share == here) & (col != block)
    ext = jnp.where(mine, place * share + inner % share, -1)
    wanted = lax.broadcasted_iota(jnp.int32, (SHARDS * share, blocks, 1), 0)
    mask = jnp.any(ext[None] == wanted, axis=2).astype(F32)
    lists = []
    for part in (mask[: 2 * share], mask[2 * share :]):
        flat = part.size
        part = part.reshape(flat)
        index = jnp.arange(flat, dtype=jnp.int32)
        upto = (index[:, None] <= index[None, :]).astype(F32)
        place = jnp.dot(part, upto).astype(jnp.int32)
        wide = jnp.arange(flat + GROUP + 1, dtype=jnp.int32)[None, :]
        used = part[:, None] > 0
        hit = (place[:, None] == wide + 1) & used
        last = (wide == flat + GROUP) & used
        lists.append(jnp.sum(jnp.where(hit, index[:, None], last.astype(jnp.int32)), axis=0))
    return lists


def local(embedding, start_block, start_step, rotations, neighbour_cols, tile_counts):
    devices = lax.axis_size("tiles")
    width = start_block.shape[1]
    share = width // BR
    blocks = tile_counts.shape[0]
    total = width * devices * lax.axis_size("rows")
    here, row = lax.axis_index("tiles"), lax.axis_index("rows")

    meta = jnp.stack([here, row % 2])
    own_emb, own_vec = call(
        pack_kernel,
        [((width, EMB), BF16), ((2 * K, width), BF16)],
        meta,
        embedding,
        start_block,
        start_step,
        smem=1,
        hbm=3,
        scratch=[
            pltpu.VMEM((K, width), F32),
            pltpu.VMEM((K, width), F32),
            pltpu.SemaphoreType.DMA((3,)),
        ],
        us=1.0,
    )
    emb_a, emb_b, emb_core = across(own_emb)
    lists = after(neighbour_cols, emb_core)
    bits = 1
    while bits < devices:
        lists = jnp.concatenate([lists, swapped(lists, "tiles", bits)], axis=1)
        bits *= 2
    items = tile_list(lists, tile_counts, here, row, share, devices)
    own_vec = after(own_vec, emb_core)
    vec_a, vec_b, vec_core = across(own_vec)
    (unit_own,) = call(
        unit_kernel,
        [((blocks, BR, EMB), BF16)],
        after(embedding.reshape(blocks, BR, EMB), emb_core),
        hbm=1,
        scratch=[pltpu.VMEM((blocks, BR, EMB), BF16), pltpu.SemaphoreType.DMA((4,))],
        us=2.6,
    )
    near, far = 2 * share * blocks, (SHARDS - 2) * share * blocks
    near_shape, far_shape = (share + near + GROUP, BR, BR), (far + GROUP, BR, BR)
    near_sems = pltpu.SemaphoreType.DMA((near // GROUP + 2,))
    diag, tiles_near = call(
        functools.partial(near_kernel, blocks, share),
        [((1, width), F32), (near_shape, BF16, "hbm")],
        meta,
        items[0],
        unit_own,
        emb_core,
        smem=2,
        scratch=[
            pltpu.VMEM((2 * share, BR, EMB), BF16),
            pltpu.VMEM(near_shape, BF16),
            near_sems,
        ],
        us=2.0,
    )
    emb_a, emb_b, vec_a, vec_b = (after(side, diag) for side in (emb_a, emb_b, vec_a, vec_b))
    parts = call(
        functools.partial(far_kernel, blocks, share, devices),
        ([((K, width), F32)] + [((K, width), BF16)] * (devices - 1)) * 2
        + [(near_shape, BF16), (far_shape, BF16)],
        meta,
        *items,
        tiles_near,
        unit_own,
        *by_core(emb_a, emb_b),
        own_vec,
        vec_core,
        *by_core(vec_a, vec_b),
        smem=3,
        hbm=1,
        scratch=[
            pltpu.VMEM(((SHARDS - 2) * share, BR, EMB), BF16),
            pltpu.VMEM((SHARDS * share, 2 * K, BR), BF16),
            pltpu.VMEM((blocks + 1, 2 * K, BR), F32),
            near_sems,
        ],
        us=5.0,
    )
    parts, tiles_near, tiles_far = parts[:-2], parts[-2], parts[-1]

    def applied(halo):
        return call(
            functools.partial(apply_kernel, blocks, share, devices),
            [((K, width), F32)] + [((K, width), BF16)] * (devices - 1),
            meta,
            *items,
            tiles_near,
            tiles_far,
            *halo,
            smem=3,
            scratch=[
                pltpu.VMEM((SHARDS * share, K, BR), BF16),
                pltpu.VMEM((blocks + 1, K, BR), F32),
            ],
            us=3.0,
        )

    def gathered(parts):
        return [parts[0]] + [rotated(part, "tiles", n + 1) for n, part in enumerate(parts[1:])]

    parts, step_out = gathered(parts[:devices]), parts[devices:]
    image, image_half = call(
        functools.partial(image_kernel, devices),
        [((K, width), F32), ((K, width), BF16)],
        *parts,
        diag,
        start_block,
        us=0.1,
    )
    image_core = swapped(image_half, "rows", 1)
    image_side = other_side(jnp.concatenate([image_half, image_core], axis=0), False)
    rows, gram = call(
        gram_kernel,
        [((3 * K, width), F32), ((3 * K, 2 * K), F32)],
        start_block,
        start_step,
        after(image, image_core),
        us=0.8,
    )
    step_parts = gathered([after(part, gram) for part in step_out])
    image_side = after(image_side, *step_parts[1:2])
    image_vec = [image_half, image_core, image_side, swapped(image_side, "rows", 1)]
    parts = gathered(applied(image_vec))
    step_image, twice, keep, send = call(
        functools.partial(twice_kernel, devices),
        [((K, width), F32)] * 2 + [((15 * K // 4, 2 * K), F32)] * 2,
        meta,
        rows,
        gram,
        start_step,
        diag,
        *step_parts,
        *parts,
        smem=1,
        us=1.3,
    )
    products = sum_chips(sum_chips(keep + swapped(send, "rows", 1), 0), 1)
    return call(
        functools.partial(last_kernel, total),
        [((K, width), F32)] * 2,
        meta,
        rotations.swapaxes(1, 2),
        rows,
        step_image,
        twice,
        products,
        swapped(products, "rows", 1),
        smem=1,
        us=3.2,
    )


def solution(mesh):
    return jax.shard_map(
        local,
        mesh=mesh,
        in_specs=(
            P("rows", None),
            P(None, ("rows", "tiles")),
            P(None, ("rows", "tiles")),
            P(),
            P("rows", "tiles"),
            P("rows"),
        ),
        out_specs=(P(None, ("rows", "tiles")), P(None, ("rows", "tiles"))),
        check_vma=False,
    )
```

```python
import functools
import math

import jax
import jax.numpy as jnp
from jax import lax
from jax.experimental import pallas as pl
from jax.experimental.pallas import tpu as pltpu
from jax.sharding import PartitionSpec as P

EMB = 256
K = 64
BR = 128
MAXT = 48
REACH = 2
ITERS = 2

TAU = 6.0
EPS = 1e-06
PRECISE = lax.Precision.HIGHEST

WEIGHT = 1.0 / (BR * MAXT)
SIGMA = math.exp(TAU) * WEIGHT
EXP2 = TAU / EMB * math.log2(math.e)
GROUP = 16
SHARDS = 6
F32 = jnp.float32
BF16 = jnp.bfloat16
VMEM = pl.BlockSpec(memory_space=pltpu.VMEM)
SMEM = pl.BlockSpec(memory_space=pltpu.SMEM)


def swapped(value, axis, bits):
    count = lax.axis_size(axis)
    return lax.ppermute(value, axis, [(i, i ^ bits) for i in range(count)])


def rotated(value, axis, steps):
    count = lax.axis_size(axis)
    return lax.ppermute(value, axis, [(i, (i + steps) % count) for i in range(count)])


def other_side(value, core_0_too=True):
    count = lax.axis_size("rows")
    chips = count // 2
    pairs = []
    for r in range(count):
        chip, core = divmod(r, 2)
        to = (chip + 1) % chips if chip % 2 else (chip - 1) % chips
        pairs.append((r, to * 2 + core if core or core_0_too else r ^ 2))
    return lax.ppermute(value, "rows", pairs)


def after(value, *others):
    return lax.optimization_barrier((value, *others))[0]


def across(value):
    return swapped(value, "rows", 2), other_side(value), swapped(value, "rows", 1)


def by_core(side_a, side_b):
    return [side_a, swapped(side_a, "rows", 1), side_b, swapped(side_b, "rows", 1)]


def sum_along(value, axis, bits):
    while bits < lax.axis_size(axis):
        value = value + swapped(value, axis, bits)
        bits *= 2
    return value


def sum_chips(value, part):
    rows, tiles = lax.axis_size("rows"), lax.axis_size("tiles")
    if rows // 2 != tiles or tiles != 4:
        return sum_along(value, "tiles", 1) if part else sum_along(value, "rows", 2)
    parts = [value]
    for step in range(1, 4):
        pairs = []
        for r in range(rows):
            for t in range(tiles):
                along_rows = r % 2 == part
                to = (r ^ (2 * step), t) if along_rows else (r, (t + step) % tiles)
                pairs.append((r * tiles + t, to[0] * tiles + to[1]))
        parts.append(lax.ppermute(value, ("rows", "tiles"), pairs))
    return sum(parts)


def dot_t(a, b):
    return lax.dot_general(a, b, (((1,), (1,)), ((), ())), preferred_element_type=F32)


def dot_exact(a, b):
    return lax.dot_general(
        a, b, (((1,), (1,)), ((), ())), precision=PRECISE, preferred_element_type=F32
    )


def unit_of(rows):
    values = rows.astype(F32)
    mean = jnp.sum(values * values, axis=-1, keepdims=True) * (1.0 / EMB)
    return (values * lax.rsqrt(mean + EPS)).astype(BF16)


def pack_kernel(meta, emb, block, step, emb_out, vec_out, block_buf, step_buf, sems):
    here, width = meta[0], emb_out.shape[0]
    copies = [
        pltpu.make_async_copy(emb.at[pl.ds(here * width, width), :], emb_out, sems.at[0]),
        pltpu.make_async_copy(block, block_buf, sems.at[1]),
        pltpu.make_async_copy(step, step_buf, sems.at[2]),
    ]
    for copy in copies:
        copy.start()
    copies[1].wait()
    vec_out[:K, :] = block_buf[...].astype(BF16)
    copies[2].wait()
    vec_out[K:, :] = step_buf[...].astype(BF16)
    copies[0].wait()


def group_copies(count, first, source, target, sems, body):
    @pl.loop(0, (count + GROUP - 1) // GROUP)
    def _(step):
        at = pl.ds(first + step * GROUP, GROUP)
        body(pltpu.make_async_copy(source.at[at], target.at[at], sems.at[step]))


def build_tiles(blocks, first, items, unit_own, unit_ext, tiles, stored=None, sems=None):
    count = items[items.shape[0] - 1]

    @pl.loop(0, (count + GROUP - 1) // GROUP)
    def _(step):
        picked = [items[step * GROUP + g] for g in range(GROUP)]
        scores = [dot_t(unit_ext[f // blocks], unit_own[f % blocks]) for f in picked]
        for g in range(GROUP):
            tiles[first + step * GROUP + g] = jnp.exp2(scores[g] * EXP2).astype(BF16)
        if stored is not None:
            at = pl.ds(first + step * GROUP, GROUP)
            pltpu.make_async_copy(tiles.at[at], stored.at[at], sems.at[step]).start()


def unit_kernel(emb, unit, buf, sems):
    blocks, parts = unit.shape[0], sems.shape[0]
    each = blocks // parts
    copies = [
        pltpu.make_async_copy(
            emb.at[pl.ds(n * each, each)], buf.at[pl.ds(n * each, each)], sems.at[n]
        )
        for n in range(parts)
    ]
    for copy in copies:
        copy.start()
    for n, copy in enumerate(copies):
        copy.wait()
        at = pl.ds(n * each, each)
        unit[at] = unit_of(buf[at])


def near_kernel(
    blocks, share, meta, items, unit_own, emb_core, diag_out, stored, unit_ext, tiles, sems
):
    here = meta[0]
    for i in range(share):
        unit_ext[i] = unit_own[here * share + i]
        unit_ext[share + i] = unit_of(emb_core[pl.ds(i * BR, BR), :])
    rows = lax.broadcasted_iota(jnp.int32, (BR, BR), 0)
    cols = lax.broadcasted_iota(jnp.int32, (BR, BR), 1)
    for i in range(share):
        unit = unit_ext[i]
        weights = jnp.exp2(dot_t(unit, unit) * EXP2)
        on_diag = rows == cols
        diag_out[:, pl.ds(i * BR, BR)] = (
            jnp.sum(jnp.where(on_diag, weights, 0.0), axis=0, keepdims=True) * WEIGHT - SIGMA
        )
        tiles[i] = jnp.where(on_diag, 0.0, weights).astype(BF16)
    at = pl.ds(0, share)
    copy = pltpu.make_async_copy(tiles.at[at], stored.at[at], sems.at[sems.shape[0] - 1])
    copy.start()
    build_tiles(blocks, share, items, unit_own, unit_ext, tiles, stored, sems)
    count = items[items.shape[0] - 1]
    group_copies(count, share, tiles, stored, sems, lambda copy: copy.wait())
    copy.wait()


def apply_tiles(blocks, share, devices, here, items, tiles, outs, vec_ext, acc):
    acc[...] = jnp.zeros_like(acc)
    for i in range(share):
        acc[here * share + i] = jnp.dot(vec_ext[i], tiles[0][i], preferred_element_type=F32)
    for part in range(2):
        count, first, base = items[part][items[part].shape[0] - 1], (share, 0)[part], (0, 2 * share)[part]

        @pl.loop(0, (count + GROUP - 1) // GROUP)
        def _(step):
            picked = []
            for g in range(GROUP):
                at = step * GROUP + g
                flat = items[part][at]
                picked.append(
                    (base + flat // blocks, jnp.where(at < count, flat % blocks, blocks))
                )
            parts = [
                jnp.dot(
                    vec_ext[ext],
                    tiles[part][first + step * GROUP + g],
                    preferred_element_type=F32,
                )
                for g, (ext, _) in enumerate(picked)
            ]
            for (_, to), value in zip(picked, parts):
                acc[to] += value

    for n, out in enumerate(outs):
        rows = pl.ds(n // devices * K, K)
        at_block = lax.rem(here + n % devices, devices) * share
        for i in range(share):
            value = acc[at_block + i, rows, :] * WEIGHT
            out[:, pl.ds(i * BR, BR)] = value.astype(out.dtype)


def far_kernel(blocks, share, devices, *refs):
    meta, items, stored, unit_own = refs[0], refs[1:3], refs[3], refs[4]
    emb, vec = refs[5 : 3 + SHARDS], refs[3 + SHARDS : 3 + 2 * SHARDS]
    outs, (near, far, unit_ext, vec_ext, acc, sems) = refs[3 + 2 * SHARDS : -6], refs[-6:]
    count, at = items[0][items[0].shape[0] - 1], pl.ds(0, share)
    copy = pltpu.make_async_copy(stored.at[at], near.at[at], sems.at[sems.shape[0] - 1])
    copy.start()
    group_copies(count, share, stored, near, sems, lambda copy: copy.start())
    for j, ref in enumerate(emb):
        for i in range(share):
            unit_ext[j * share + i] = unit_of(ref[pl.ds(i * BR, BR), :])
    build_tiles(blocks, 0, items[1], unit_own, unit_ext, far)
    copy.wait()
    group_copies(count, share, stored, near, sems, lambda copy: copy.wait())
    for j, ref in enumerate(vec):
        for i in range(share):
            vec_ext[j * share + i] = ref[:, pl.ds(i * BR, BR)]
    apply_tiles(blocks, share, devices, meta[0], items, (near, far), outs, vec_ext, acc)


def apply_kernel(blocks, share, devices, *refs):
    meta, items, tiles = refs[0], refs[1:3], refs[3:5]
    own, core, mine, other = refs[5:9]
    outs, (vec_ext, acc) = refs[9:-2], refs[-2:]
    odd = meta[1]
    slots = [(own, 0, 0), (core, 0, 1)]
    slots += [(mine, 0, 2 + 2 * odd), (mine, 1, 3 + 2 * odd)]
    slots += [(other, 0, 5 - 2 * odd), (other, 1, 4 - 2 * odd)]
    for ref, half, slot in slots:
        for i in range(share):
            vec_ext[slot * share + i] = ref[pl.ds(half * K, K), pl.ds(i * BR, BR)]
    apply_tiles(blocks, share, devices, meta[0], items, tiles, outs, vec_ext, acc)


def summed(parts, diag, vectors):
    value = parts[0][...] + diag[...] * vectors
    for ref in parts[1:]:
        value = value + ref[...].astype(F32)
    return value


def image_kernel(devices, *refs):
    parts, (diag, vec, out, out_half) = refs[:devices], refs[devices:]
    value = summed(parts, diag, vec[...])
    out[...] = value
    out_half[...] = value.astype(BF16)


def mul(a, b):
    return jnp.dot(a, b, precision=PRECISE, preferred_element_type=F32)


def halves_of(value):
    high = value.astype(BF16)
    return high, (value - high.astype(F32)).astype(BF16)


def mul3(a, b):
    (a_high, a_low), (b_high, b_low) = halves_of(a), halves_of(b)
    return jnp.dot(
        jnp.concatenate([a_high, a_high, a_low], axis=1),
        jnp.concatenate([b_high, b_low, b_high], axis=0),
        preferred_element_type=F32,
    )


def dot3(a, b):
    (a_high, a_low), (b_high, b_low) = halves_of(a), halves_of(b)
    return dot_t(
        jnp.concatenate([a_high, a_high, a_low], axis=1),
        jnp.concatenate([b_high, b_low, b_high], axis=1),
    )


def eye_mask(n):
    shape = (n, n)
    return lax.broadcasted_iota(jnp.int32, shape, 0) == lax.broadcasted_iota(jnp.int32, shape, 1)


def as_row(column):
    return jnp.sum(jnp.where(eye_mask(K), column, 0.0), axis=0, keepdims=True)


def step_coefficients(g_vv, g_vs, g_ss, g_jv, g_js, g_jj, rotation, total):
    m_t = g_jv * (1.0 / total) + SIGMA * (g_vv * (1.0 / total) - eye_mask(K).astype(F32))
    resid_sq = jnp.sum(
        jnp.where(eye_mask(K), g_jj, 0.0) + m_t * (mul(m_t, g_vv) - 2.0 * g_jv),
        axis=1,
        keepdims=True,
    )
    resid_inv = 1.0 / jnp.sqrt(jnp.maximum(resid_sq, 0.0) * (1.0 / total) + EPS)
    on_v, on_resid, on_s = rotation[:, :K], rotation[:, K : 2 * K], rotation[:, 2 * K :]
    p_j = on_resid * as_row(resid_inv)
    p_step = -mul3(p_j, m_t)
    coef = jnp.concatenate(
        [
            jnp.concatenate([on_v + p_step, on_s, p_j], axis=1),
            jnp.concatenate([p_step, on_s, p_j], axis=1),
        ],
        axis=0,
    )
    gram = jnp.concatenate(
        [
            jnp.concatenate([g_vv, g_vs, g_jv.T], axis=1),
            jnp.concatenate([g_vs.T, g_ss, g_js.T], axis=1),
            jnp.concatenate([g_jv, g_js, g_jj], axis=1),
        ],
        axis=0,
    )
    on_gram = mul3(coef, gram)
    comb_sq = jnp.sum(on_gram[:K] * coef[:K], axis=1, keepdims=True)
    scale = 1.0 / jnp.sqrt(jnp.maximum(comb_sq, 0.0) * (1.0 / total) + EPS)
    return coef, on_gram, jnp.concatenate([scale, scale], axis=0)


def split_by_core(core, value, keep, send):
    half = keep.shape[0]
    keep[...] = jnp.where(core == 0, value[:half], value[half:])
    send[...] = jnp.where(core == 0, value[half:], value[:half])


def joined(core, mine, other):
    return jnp.concatenate(
        [
            jnp.where(core == 0, mine[...], other[...]),
            jnp.where(core == 0, other[...], mine[...]),
        ],
        axis=0,
    )


def gram_kernel(x_ref, y_ref, j_ref, rows, out):
    rows[:K, :] = x_ref[...]
    rows[K : 2 * K, :] = y_ref[...]
    rows[2 * K :, :] = j_ref[...]
    g = dot_exact(rows[...], rows[...])
    out[:K, :] = g[:K, : 2 * K]
    out[K : 2 * K, :K] = g[K : 2 * K, K : 2 * K]
    out[K : 2 * K, K:] = g[2 * K :, 2 * K :]
    out[2 * K :, :] = g[2 * K :, : 2 * K]


def first_step(packed, rotation, total):
    xx, xy = packed[:K, :K], packed[:K, K:]
    yy, jj = packed[K : 2 * K, :K], packed[K : 2 * K, K:]
    jx, jy = packed[2 * K :, :K], packed[2 * K :, K:]

    def inv_rms(square):
        picked = jnp.sum(jnp.where(eye_mask(K), square, 0.0), axis=1, keepdims=True)
        return 1.0 / jnp.sqrt(picked * (1.0 / total) + EPS)

    x_col, y_col = inv_rms(xx), inv_rms(yy)
    x_row, y_row = as_row(x_col), as_row(y_col)
    coef, on_gram, scale = step_coefficients(
        xx * x_col * x_row,
        xy * x_col * y_row,
        yy * y_col * y_row,
        jx * x_col * x_row,
        jy * x_col * y_row,
        jj * x_col * x_row,
        rotation,
        total,
    )
    coef = scale * coef
    gram = dot3(scale * on_gram, coef)
    coef = coef * jnp.concatenate([x_row, y_row, x_row], axis=1)
    return coef, gram, mul3(coef[:K, :K], jnp.concatenate([jx, jy, jj], axis=1))


def twice_kernel(devices, meta, rows, gram, step, diag, *refs):
    t_parts, q_parts = refs[:devices], refs[devices : 2 * devices]
    t_out, q_out, keep, send = refs[2 * devices :]
    t = summed(t_parts, diag, step[...])
    q = summed(q_parts, diag, rows[2 * K :, :])
    t_out[...] = t
    q_out[...] = q
    both = jnp.concatenate([t, q], axis=0)
    on_rows = dot3(both, rows[...])
    on_both = dot3(both, both)
    half = K // 2
    packed = jnp.concatenate(
        [
            gram[...],
            on_rows[:, : 2 * K],
            jnp.concatenate([on_rows[:K, 2 * K :], on_rows[K:, 2 * K :]], axis=1),
            on_both[K:],
            jnp.concatenate([on_both[:half, :K], on_both[half:K, :K]], axis=1),
        ],
        axis=0,
    )
    split_by_core(meta[1], packed, keep, send)


def deep_kernel(rows, t_ref, q_ref, out):
    high, low = halves_of(jnp.concatenate([rows[...], t_ref[...], q_ref[...]], axis=0))
    depth = high.shape[0]
    out[:depth, :] = high
    out[depth : 2 * depth, :] = low
    out[2 * depth :, :] = high


def last_kernel(total, meta, rot_ref, deep, mine, other, v_out, s_out):
    packed = joined(meta[1], mine, other)
    coef, gram, known = first_step(packed[: 3 * K], rot_ref[0], total)
    packed = packed[3 * K :]
    on_xy, on_j, on_both = packed[: 2 * K], packed[2 * K : 3 * K], packed[3 * K :]
    tq_j = jnp.concatenate([on_j[:, :K], on_j[:, K:]], axis=0)
    qt, qq = on_both[:K, :K], on_both[:K, K:]
    tt = jnp.concatenate([on_both[K:, :K], on_both[K:, K:]], axis=0)
    on_tq = jnp.concatenate(
        [jnp.concatenate([tt, qt.T], axis=1), jnp.concatenate([qt, qq], axis=1)], axis=0
    )
    image = mul3(coef[:K, K:], jnp.concatenate([on_xy, tq_j, on_tq], axis=1))
    on_rows = known + image[:, : 3 * K]
    on_tq = dot3(coef[:K, :K], tq_j) + image[:, 3 * K :]
    j_new = dot3(on_rows, coef)
    g_jj = dot3(jnp.concatenate([on_rows[:, 2 * K :], on_tq], axis=1), coef[:K])
    again, _, scale = step_coefficients(
        gram[:K, :K],
        gram[:K, K:],
        gram[K:, K:],
        j_new[:, :K],
        j_new[:, K:],
        g_jj,
        rot_ref[1],
        total,
    )
    on_new = mul3(again[:, : 2 * K], coef)
    on_image = mul3(again[:, 2 * K :], coef[:K])
    both = jnp.concatenate(
        [
            on_new[:, : 2 * K],
            on_new[:, 2 * K :] + on_image[:, :K],
            on_image[:, K:],
        ],
        axis=1,
    )
    high, low = halves_of(both)
    both = scale * jnp.dot(
        jnp.concatenate([high, high, low], axis=1), deep[...], preferred_element_type=F32
    )
    v_out[...], s_out[...] = both[:K], both[K:]


def call(kernel, outs, *args, smem=0, hbm=0, scratch=(), us=0.0):
    any_memory = pl.BlockSpec(memory_space=pl.ANY)
    args = [
        pltpu.with_memory_space_constraint(arg, pltpu.HBM) if smem <= n < smem + hbm else arg
        for n, arg in enumerate(args)
    ]
    return pl.pallas_call(
        kernel,
        out_shape=tuple(
            pltpu.HBM(*out[:2]) if len(out) > 2 else jax.ShapeDtypeStruct(*out) for out in outs
        ),
        in_specs=[SMEM] * smem + [any_memory] * hbm + [VMEM] * (len(args) - smem - hbm),
        out_specs=tuple(any_memory if len(out) > 2 else VMEM for out in outs),
        scratch_shapes=list(scratch),
        compiler_params=pltpu.CompilerParams(vmem_limit_bytes=16 * 1024 * 1024),
        cost_estimate=pl.CostEstimate(
            flops=int(us * 1e9), bytes_accessed=0, transcendentals=0
        ),
    )(*args)


def tile_list(cols, counts, here, row, share, devices):
    blocks, span = cols.shape[0], cols.shape[1] // devices
    slot = jnp.concatenate(
        [
            (here ^ n) * span + lax.broadcasted_iota(jnp.int32, (blocks, span), 1)
            for n in range(devices)
        ],
        axis=1,
    )
    col = cols
    block = row * blocks + lax.broadcasted_iota(jnp.int32, col.shape, 0)
    shard, inner = col // blocks, col % blocks
    other_core = (shard % 2 != row % 2).astype(jnp.int32)
    chip, own_chip = shard // 2, row // 2
    place = other_core + jnp.where(chip == own_chip, 0, jnp.where(chip == own_chip ^ 1, 2, 4))
    mine = (slot < counts[:, None]) & (inner // share == here) & (col != block)
    ext = jnp.where(mine, place * share + inner % share, -1)
    wanted = lax.broadcasted_iota(jnp.int32, (SHARDS * share, blocks, 1), 0)
    mask = jnp.any(ext[None] == wanted, axis=2).astype(F32)
    lists = []
    for part in (mask[: 2 * share], mask[2 * share :]):
        flat = part.size
        part = part.reshape(flat)
        index = jnp.arange(flat, dtype=jnp.int32)
        upto = (index[:, None] <= index[None, :]).astype(F32)
        place = jnp.dot(part, upto).astype(jnp.int32)
        wide = jnp.arange(flat + GROUP + 1, dtype=jnp.int32)[None, :]
        used = part[:, None] > 0
        hit = (place[:, None] == wide + 1) & used
        last = (wide == flat + GROUP) & used
        lists.append(jnp.sum(jnp.where(hit, index[:, None], last.astype(jnp.int32)), axis=0))
    return lists


def local(embedding, start_block, start_step, rotations, neighbour_cols, tile_counts):
    devices = lax.axis_size("tiles")
    width = start_block.shape[1]
    share = width // BR
    blocks = tile_counts.shape[0]
    total = width * devices * lax.axis_size("rows")
    here, row = lax.axis_index("tiles"), lax.axis_index("rows")

    meta = jnp.stack([here, row % 2])
    own_emb, own_vec = call(
        pack_kernel,
        [((width, EMB), BF16), ((2 * K, width), BF16)],
        meta,
        embedding,
        start_block,
        start_step,
        smem=1,
        hbm=3,
        scratch=[
            pltpu.VMEM((K, width), F32),
            pltpu.VMEM((K, width), F32),
            pltpu.SemaphoreType.DMA((3,)),
        ],
        us=1.0,
    )
    emb_a, emb_b, emb_core = across(own_emb)
    lists = after(neighbour_cols, emb_core)
    bits = 1
    while bits < devices:
        lists = jnp.concatenate([lists, swapped(lists, "tiles", bits)], axis=1)
        bits *= 2
    items = tile_list(lists, tile_counts, here, row, share, devices)
    own_vec = after(own_vec, emb_core)
    vec_a, vec_b, vec_core = across(own_vec)
    (unit_own,) = call(
        unit_kernel,
        [((blocks, BR, EMB), BF16)],
        after(embedding.reshape(blocks, BR, EMB), emb_core),
        hbm=1,
        scratch=[pltpu.VMEM((blocks, BR, EMB), BF16), pltpu.SemaphoreType.DMA((4,))],
        us=2.6,
    )
    near, far = 2 * share * blocks, (SHARDS - 2) * share * blocks
    near_shape, far_shape = (share + near + GROUP, BR, BR), (far + GROUP, BR, BR)
    near_sems = pltpu.SemaphoreType.DMA((near // GROUP + 2,))
    diag, tiles_near = call(
        functools.partial(near_kernel, blocks, share),
        [((1, width), F32), (near_shape, BF16, "hbm")],
        meta,
        items[0],
        unit_own,
        emb_core,
        smem=2,
        scratch=[
            pltpu.VMEM((2 * share, BR, EMB), BF16),
            pltpu.VMEM(near_shape, BF16),
            near_sems,
        ],
        us=2.0,
    )
    emb_a, emb_b, vec_a, vec_b = (after(side, diag) for side in (emb_a, emb_b, vec_a, vec_b))
    parts = call(
        functools.partial(far_kernel, blocks, share, devices),
        ([((K, width), F32)] + [((K, width), BF16)] * (devices - 1)) * 2
        + [(near_shape, BF16), (far_shape, BF16)],
        meta,
        *items,
        tiles_near,
        unit_own,
        *by_core(emb_a, emb_b),
        own_vec,
        vec_core,
        *by_core(vec_a, vec_b),
        smem=3,
        hbm=1,
        scratch=[
            pltpu.VMEM(((SHARDS - 2) * share, BR, EMB), BF16),
            pltpu.VMEM((SHARDS * share, 2 * K, BR), BF16),
            pltpu.VMEM((blocks + 1, 2 * K, BR), F32),
            near_sems,
        ],
        us=5.0,
    )
    parts, tiles_near, tiles_far = parts[:-2], parts[-2], parts[-1]

    def applied(halo):
        return call(
            functools.partial(apply_kernel, blocks, share, devices),
            [((K, width), F32)] + [((K, width), BF16)] * (devices - 1),
            meta,
            *items,
            tiles_near,
            tiles_far,
            *halo,
            smem=3,
            scratch=[
                pltpu.VMEM((SHARDS * share, K, BR), BF16),
                pltpu.VMEM((blocks + 1, K, BR), F32),
            ],
            us=3.0,
        )

    def gathered(parts):
        return [parts[0]] + [rotated(part, "tiles", n + 1) for n, part in enumerate(parts[1:])]

    parts, step_out = gathered(parts[:devices]), parts[devices:]
    image, image_half = call(
        functools.partial(image_kernel, devices),
        [((K, width), F32), ((K, width), BF16)],
        *parts,
        diag,
        start_block,
        us=0.1,
    )
    image_core = swapped(image_half, "rows", 1)
    image_side = other_side(jnp.concatenate([image_half, image_core], axis=0), False)
    rows, gram = call(
        gram_kernel,
        [((3 * K, width), F32), ((3 * K, 2 * K), F32)],
        start_block,
        start_step,
        after(image, image_core),
        us=0.8,
    )
    step_parts = gathered([after(part, gram) for part in step_out])
    image_side = after(image_side, *step_parts[1:2])
    image_vec = [image_half, image_core, image_side, swapped(image_side, "rows", 1)]
    parts = gathered(applied(image_vec))
    step_image, twice, keep, send = call(
        functools.partial(twice_kernel, devices),
        [((K, width), F32)] * 2 + [((15 * K // 4, 2 * K), F32)] * 2,
        meta,
        rows,
        gram,
        start_step,
        diag,
        *step_parts,
        *parts,
        smem=1,
        us=1.3,
    )
    (deep,) = call(
        deep_kernel, [((15 * K, width), BF16)], rows, step_image, twice, us=0.5
    )
    products = sum_chips(sum_chips(keep + swapped(send, "rows", 1), 0), 1)
    return call(
        functools.partial(last_kernel, total),
        [((K, width), F32)] * 2,
        meta,
        rotations.swapaxes(1, 2),
        deep,
        products,
        swapped(products, "rows", 1),
        smem=1,
        us=3.2,
    )


def solution(mesh):
    return jax.shard_map(
        local,
        mesh=mesh,
        in_specs=(
            P("rows", None),
            P(None, ("rows", "tiles")),
            P(None, ("rows", "tiles")),
            P(),
            P("rows", "tiles"),
            P("rows"),
        ),
        out_specs=(P(None, ("rows", "tiles")), P(None, ("rows", "tiles"))),
        check_vma=False,
    )
```
